32 devices in a mesh: groups: 2 (over x), attn: 16 (over z, y, core).
Axes of the slice: x: 2, y: 2, z: 4, core: 2. Of those that a mesh axis runs over, the one named last changes fastest.
Arguments:
- hidden_states: bfloat16 [16, 16384], P('groups', 'attn'), parts along dimension 0, may hold values from -6 to 6
- norm_gain: float32 [16384], replicated, may hold values from 0.1 to 1.9
- w_query: bfloat16 [16384, 8192], P(None, 'attn'), may hold values from -0.046875 to 0.046875
- w_kv: bfloat16 [16384, 1024], P('attn'), may hold values from -0.046875 to 0.046875
- w_out: bfloat16 [8192, 16384], P('attn'), may hold values from -0.5 to 0.5
- k_cache: bfloat16 [1152, 128, 128], P(('groups', 'attn')), parts along dimension 0, may hold values from -130 to 130
- v_cache: bfloat16 [1152, 128, 128], P(('groups', 'attn')), parts along dimension 0, may hold values from -6 to 6
- block_table: int32 [16, 4, 32], P('groups'), parts along dimension 0, may hold values from -1 to 575, as said below
- lengths: int32 [16], P('groups'), parts along dimension 0, may hold values from 1 to 4096, as said below
Outputs:
- attn_out: bfloat16 [16, 16384], P('groups', 'attn'), parts along dimension 0
- new_entries: bfloat16 [16, 1024], P('groups'), parts along dimension 0
The draws below stay inside these ranges and needn't reach their ends.
There are 2 independent parts, one for each index of `groups`. The reference program is written for one: setup_inputs(seed, part) draws one part's arguments, and reference() takes and returns one part's arrays. A program takes and returns all parts, laid end to end along the dimension named above; an argument that names none is the same for every part. Nothing has to cross between parts.
Inputs may be any that keep to these rules, and one draw needn't show every extreme that they name: `lengths`: every request has one to 2048 positions except one request that has exactly 4096. `block_table`: entry [r, g, p] is the global slot (device index along attn times 36 plus local slot) holding page p of request r and key-value head g when p * 128 < lengths[r], and -1 otherwise; no slot is named twice. The slots of one request, all key-value heads together, are consecutive modulo 576: head by head, pages in order.
All inputs are finite; a program needn't handle non-finite values.
Results may differ from the reference program's by a relative error of at most 0.0055.
The reference program's roundings to bfloat16 on the way (of `normed`, `queries` and `attention`) count: a program that leaves them out, or rounds other values in their place, can miss the bound.
Values may be sent and summed in bfloat16 or wider, within the bound.
No kernel may reach another device: no remote copies, remote signals or barrier semaphores. Data moves between devices by JAX's collectives and lax.ppermute only.
A program may use at most 128 MiB of HBM per device.

```python
import math
import jax
import jax.numpy as jnp
from jax import lax

D = 16384
HD = 128
H = 64
KVH = 4
PAGE = 128
CTX_MAX = 4096
REQ = 8
PAGES = 32
SLOTS = 576


def request_layout(key):
    first_key, second_key, third_key, fourth_key = jax.random.split(key, 4)
    short_lengths = jax.random.randint(first_key, (REQ,), 1, CTX_MAX // 2 + 1)
    longest = jax.random.randint(second_key, (), 0, REQ)
    context = jnp.where(jnp.arange(REQ) == longest, CTX_MAX, short_lengths).astype(jnp.int32)
    return (context, third_key, fourth_key)


def draw_lengths(key, part):
    context, unused_a, unused_b = request_layout(key)
    return context


def draw_block_table(key, part):
    context, order_key, offset_key = request_layout(key)
    page_need = (context + PAGE - 1) // PAGE
    order = jax.random.permutation(order_key, REQ)
    ranking = jnp.zeros((REQ,), jnp.int32).at[order].set(jnp.arange(REQ, dtype=jnp.int32))
    count = page_need * KVH
    before = jnp.sum(count[None, :] * (ranking[None, :] < ranking[:, None]).astype(jnp.int32), axis=1)
    used = jnp.sum(count)
    offset = SLOTS - 1 - jax.random.randint(offset_key, (), 0, used)
    page_index = jnp.arange(PAGES, dtype=jnp.int32)
    head_index = jnp.arange(KVH, dtype=jnp.int32)
    inside = head_index[None, :, None] * page_need[:, None, None] + page_index[None, None, :]
    slot = (before[:, None, None] + inside + offset) % SLOTS
    valid = page_index[None, None, :] < page_need[:, None, None]
    return jnp.where(valid, slot, -1).astype(jnp.int32)


def draw_k_cache(key, part):
    key = jax.random.fold_in(key, 11)
    value_key = jax.random.fold_in(key, 0)
    shape = (SLOTS, PAGE, HD)
    values = jnp.clip(1.5 * jax.random.normal(value_key, shape, jnp.float32), -9.0, 9.0)
    return values.astype(jnp.bfloat16)


def block_scale(own_key, dims, cuts, least, largest):
    def one(dim, parts):
        steps = jax.random.uniform(jax.random.fold_in(jax.random.fold_in(own_key, 6), dim), (parts,), jnp.float32, least / len(cuts), largest / len(cuts))
        return jnp.repeat(jnp.exp(steps), dims[dim] // parts).reshape((-1,) + (1,) * (len(dims) - dim - 1))

    loudness = one(*cuts[0])
    for cut in cuts[1:]:
        loudness = loudness * one(*cut)
    return loudness


def centred(stream_key, dims, scale, most, cuts=(), kind=jnp.bfloat16):
    result = jax.random.normal(stream_key, dims, jnp.float32) * scale
    if len(cuts) > 0:
        result = block_scale(stream_key, dims, cuts, -0.22, 0.18) * result
    return jnp.clip(result, min=-most, max=most).astype(kind)


def setup_inputs(seed: int = 0, part: int = 0) -> dict:
    key_list = jax.random.split(jax.random.key(seed), 10)
    part_splits = jax.random.split(jax.random.fold_in(key_list[9], part), 10)
    return {
        "hidden_states": centred(part_splits[0], (REQ, D), 1.0, 6.0, ((1, 16),)),
        "norm_gain": jnp.clip(1.0 + 0.18 * jax.random.normal(key_list[1], (D,), jnp.float32), 0.1, 1.9),
        "w_query": centred(key_list[2], (D, H * HD), D ** -0.5, 0.046875, ((1, 16),)),
        "w_kv": centred(key_list[3], (D, 2 * KVH * HD), D ** -0.5, 0.046875, ((0, 16),)),
        "w_out": centred(key_list[4], (H * HD, D), HD ** -0.5, 0.5, ((0, 16),)),
        "k_cache": draw_k_cache(jax.random.fold_in(jax.random.fold_in(key_list[9], part), 71), part),
        "v_cache": centred(part_splits[6], (SLOTS, PAGE, HD), 1.0, 6.0, ((0, 16),)),
        "block_table": draw_block_table(jax.random.fold_in(jax.random.fold_in(key_list[9], part), 71), part),
        "lengths": draw_lengths(jax.random.fold_in(jax.random.fold_in(key_list[9], part), 71), part),
    }


lowest = -1e+30
rope_base = 500000.0

def normalize(states, norm_gain):
    values = states.astype(jnp.float32)
    square_mean = lax.optimization_barrier(jnp.mean(values * values, axis=-1, keepdims=True))
    return (values * lax.rsqrt(square_mean + 1e-05) * norm_gain).astype(jnp.bfloat16)

def rotate(vectors, position):
    half_size = vectors.shape[-1] // 2
    freqs = jnp.exp(jnp.arange(half_size, dtype=jnp.float32) * (-2.0 * math.log(rope_base) / vectors.shape[-1]))
    angles = position[:, None, None] * freqs[None, None, :]
    cosine = jnp.cos(angles)
    sine = jnp.sin(angles)
    first = vectors[..., :half_size]
    second = vectors[..., half_size:]
    return jnp.concatenate([first * cosine - second * sine, second * cosine + first * sine], axis=-1)

def reference(hidden_states, norm_gain, w_query, w_kv, w_out, k_cache, v_cache, block_table, lengths):
    group_heads = H // KVH
    score_scale = 1.0 / math.sqrt(HD)
    normed = normalize(hidden_states, norm_gain)
    position = (lengths - 1).astype(jnp.float32)
    queries = rotate(jnp.dot(normed, w_query, preferred_element_type=jnp.float32).reshape(REQ, H, HD), position).astype(jnp.bfloat16)
    key_value = jnp.dot(normed, w_kv, preferred_element_type=jnp.float32)
    new_keys = rotate(key_value[:, :KVH * HD].reshape(REQ, KVH, HD), position).astype(jnp.bfloat16)
    new_values = key_value[:, KVH * HD:].reshape(REQ, KVH, HD).astype(jnp.bfloat16)
    new_entries = jnp.concatenate([new_keys.reshape(REQ, KVH * HD), new_values.reshape(REQ, KVH * HD)], axis=1)

    def per_request(items):
        query, key_new, value_new, table, length = items
        pages = jnp.maximum(table, 0)
        keys = k_cache[pages].astype(jnp.float32)
        values = v_cache[pages].astype(jnp.float32)
        grouped = query.reshape(KVH, group_heads, HD).astype(jnp.float32)
        scores = jnp.einsum('gjd,gptd->gjpt', grouped, keys) * score_scale
        places = jnp.arange(PAGES)[:, None] * PAGE + jnp.arange(PAGE)[None, :]
        live = places < length - 1
        peaks = lax.optimization_barrier(jnp.max(jnp.where(live, scores, lowest), axis=-1))
        weights = jnp.where(live, jnp.exp(scores - peaks[..., None]), 0.0)
        totals = lax.optimization_barrier(jnp.sum(weights, axis=-1))
        rounded = lax.optimization_barrier(weights.astype(jnp.bfloat16)).astype(jnp.float32)
        partial_out = jnp.einsum('gjpt,gptd->gjpd', rounded, values)
        new_score = jnp.einsum('gjd,gd->gj', grouped, key_new.astype(jnp.float32)) * score_scale
        top = jnp.maximum(lax.optimization_barrier(jnp.max(peaks, axis=-1)), new_score)
        page_weight = jnp.exp(peaks - top[..., None])
        new_weight = jnp.exp(new_score - top)
        total = lax.optimization_barrier(jnp.sum(totals * page_weight, axis=-1)) + new_weight
        mixed = lax.optimization_barrier(jnp.sum(partial_out * page_weight[..., None], axis=2)) + new_weight[..., None] * value_new.astype(jnp.float32)[:, None, :]
        return (mixed / total[..., None]).reshape(H * HD).astype(jnp.bfloat16)
    attention = lax.map(per_request, (queries, new_keys, new_values, block_table, lengths))
    attn_out = jnp.dot(attention, w_out, preferred_element_type=jnp.float32).astype(jnp.bfloat16)
    return (attn_out, new_entries)
```

```python
import math

import jax
import jax.numpy as jnp
from jax import lax
from jax.sharding import PartitionSpec as P

HD = 128
H = 64
KVH = 4
GH = H // KVH

lowest = -1e30
rope_base = 500000.0
score_scale = 1.0 / math.sqrt(HD)
bf16 = jnp.bfloat16
f32 = jnp.float32


def rope_tables(position):
    half = HD // 2
    freqs = jnp.exp(jnp.arange(half, dtype=f32) * (-2.0 * math.log(rope_base) / HD))
    angles = position[:, None] * freqs[None, :]
    cosine, sine = jnp.cos(angles), jnp.sin(angles)
    return jnp.concatenate([cosine, cosine], 1), jnp.concatenate([-sine, sine], 1)


def rotate(vectors, cosine, sine):
    return vectors * cosine + jnp.roll(vectors, HD // 2, axis=-1) * sine


def pieces(value, count):
    out = []
    for _ in range(count):
        piece = lax.reduce_precision(value, 8, 7)
        out.append(piece.astype(bf16))
        value = value - piece
    return out


def exchange(buffer):
    return lax.all_to_all(buffer, "attn", 0, 0, tiled=True)


def local(hidden, gain, w_query, w_kv, w_out, k_cache, v_cache, block_table, lengths):
    device = lax.axis_index("attn")
    n = lax.axis_size("attn")
    requests, width = hidden.shape
    columns = w_query.shape[1]
    heads = columns // HD
    slots, page = k_cache.shape[:2]
    pages = block_table.shape[2]
    pairs = requests * KVH
    assert 2 * requests == n

    hs = exchange(jnp.broadcast_to(hidden[None], (n, requests, width)))
    values = hs.astype(f32)
    square = jnp.sum(values * values, axis=(0, 2)) / (n * width)
    scale = lax.rsqrt(square + 1e-05)
    normed = (values * scale[None, :, None] * gain.reshape(n, 1, width)).astype(bf16)
    own = lax.dynamic_index_in_dim(normed, device, 0, keepdims=False)
    normed = normed.transpose(1, 0, 2).reshape(requests, n * width)

    kv = jnp.dot(own, w_kv, preferred_element_type=f32)
    position = (lengths - 1).astype(f32)
    cosine, sine = rope_tables(position)
    query = jnp.dot(normed, w_query, preferred_element_type=f32).reshape(requests, heads, HD)
    query = rotate(query, cosine[:, None], sine[:, None]).astype(bf16)
    flat_query = query.reshape(requests, columns)

    kv_rows = kv.reshape(n, KVH, HD)
    kv_block = jnp.concatenate(pieces(kv_rows, 2), axis=1)
    kv_block = jnp.pad(kv_block, ((0, 0), (0, requests - 2 * KVH), (0, 0)))
    send = jnp.concatenate(
        [jnp.broadcast_to(flat_query[None], (n, requests, columns)), kv_block], axis=2
    )
    got = exchange(send)

    kv_sum = jnp.sum(got[:, : 2 * KVH, columns:].astype(f32), axis=0)
    kv_sum = kv_sum[:KVH] + kv_sum[KVH:]
    own_request = device // 2
    turned = rotate(kv_sum, cosine[own_request][None], sine[own_request][None])
    kv_row = jnp.where(device % 2 == 0, turned, kv_sum).astype(bf16)

    queries = got[:, :, :columns].reshape(n, requests, heads, HD).transpose(1, 0, 2, 3)
    queries = queries.reshape(pairs, GH, HD)
    slot_ids = device * slots + jnp.arange(slots, dtype=jnp.int32)
    matches = block_table.reshape(-1)[None, :] == slot_ids[:, None]
    in_use = jnp.any(matches, axis=1)
    entry = jnp.sum(
        jnp.where(matches, jnp.arange(matches.shape[1], dtype=jnp.int32)[None, :], 0), axis=1
    )
    pair_of = entry // pages
    live_count = jnp.where(
        in_use, jnp.repeat(lengths, KVH)[pair_of] - 1 - (entry % pages) * page, 0
    )
    scores = (
        jnp.einsum("sjd,std->sjt", queries[pair_of], k_cache, preferred_element_type=f32)
        * score_scale
    )
    live = (jnp.arange(page, dtype=jnp.int32)[None, :] < live_count[:, None])[:, None, :]
    peak = jnp.max(jnp.where(live, scores, lowest), axis=-1)
    weights = jnp.where(live, jnp.exp(scores - peak[..., None]), 0.0)
    total = jnp.sum(weights, axis=-1)
    out = jnp.einsum("sjt,std->sjd", weights.astype(bf16), v_cache, preferred_element_type=f32)
    belongs = (jnp.arange(pairs, dtype=jnp.int32)[:, None] == pair_of[None, :]) & in_use[None, :]
    pair_peak = jnp.max(jnp.where(belongs[:, :, None], peak[None], lowest), axis=1)
    factor = jnp.exp(peak - pair_peak[pair_of])
    belongs = belongs.astype(f32)
    highest = lax.Precision.HIGHEST
    pair_total = jnp.einsum("ks,sj->kj", belongs, total * factor, precision=highest)
    pair_out = jnp.einsum("ks,sjd->kjd", belongs, out * factor[..., None], precision=highest)

    def by_head(array):
        return array.reshape((requests, n, heads) + array.shape[2:]).swapaxes(0, 1)

    stats = jnp.concatenate(
        pieces(by_head(pair_peak), 3) + pieces(by_head(pair_total), 3), axis=2
    )
    stats = jnp.pad(stats, ((0, 0), (0, 0), (0, HD // 2 - 6 * heads)))
    kv_lanes = jnp.concatenate([kv_row[:, : HD // 2], kv_row[:, HD // 2 :]], axis=0)
    kv_lanes = jnp.pad(kv_lanes, ((0, requests - 2 * KVH), (0, 0)))
    send = jnp.concatenate(
        [
            by_head(pair_out).astype(bf16).reshape(n, requests, columns),
            stats,
            jnp.broadcast_to(kv_lanes[None], (n,) + kv_lanes.shape),
        ],
        axis=2,
    )
    got = exchange(send)

    kv_lanes = got[:, : 2 * KVH, columns + HD // 2 :].reshape(requests, 2, 2, KVH, HD // 2)
    entries = kv_lanes.transpose(0, 1, 3, 2, 4).reshape(requests, 2, KVH, HD)
    new_entries = entries.reshape(requests, 2 * KVH * HD)
    group_of = (device * heads + jnp.arange(heads, dtype=jnp.int32)) // GH
    own_keys, own_values = entries[:, 0][:, group_of], entries[:, 1][:, group_of].astype(f32)
    new_score = jnp.sum(query.astype(f32) * own_keys.astype(f32), axis=-1) * score_scale
    parts_out = got[:, :, :columns].reshape(n, requests, heads, HD).astype(f32)
    parts = got[:, :, columns : columns + 6 * heads].reshape(n, requests, 6, heads).astype(f32)
    parts_peak = parts[:, :, 0] + parts[:, :, 1] + parts[:, :, 2]
    parts_total = parts[:, :, 3] + parts[:, :, 4] + parts[:, :, 5]
    top = jnp.maximum(jnp.max(parts_peak, axis=0), new_score)
    part_weight = jnp.exp(parts_peak - top[None])
    new_weight = jnp.exp(new_score - top)
    total = jnp.sum(parts_total * part_weight, axis=0) + new_weight
    mixed = jnp.sum(parts_out * part_weight[..., None], axis=0) + new_weight[..., None] * own_values
    attention = (mixed / total[..., None]).astype(bf16).reshape(requests, columns)
    terms = jnp.dot(attention, w_out, preferred_element_type=f32).astype(bf16)
    got = exchange(terms.reshape(requests, n, width).swapaxes(0, 1))
    attn_out = jnp.sum(got.astype(f32), axis=0).astype(bf16)
    return attn_out, new_entries


def solution(mesh):
    in_specs = (
        P("groups", "attn"),
        P(),
        P(None, "attn"),
        P("attn", None),
        P("attn", None),
        P(("groups", "attn"), None, None),
        P(("groups", "attn"), None, None),
        P("groups", None, None),
        P("groups"),
    )
    out_specs = (P("groups", "attn"), P("groups", None))
    return jax.shard_map(local, mesh=mesh, in_specs=in_specs, out_specs=out_specs, check_vma=False)
```

```python
import functools
import math

import jax
import jax.numpy as jnp
from jax import lax
from jax.experimental import pallas as pl
from jax.experimental.pallas import tpu as pltpu
from jax.sharding import PartitionSpec as P

HD = 128
H = 64
KVH = 4
GH = H // KVH

lowest = -1e30
rope_base = 500000.0
score_scale = 1.0 / math.sqrt(HD)
bf16 = jnp.bfloat16
f32 = jnp.float32
VMEM = pltpu.MemorySpace.VMEM
SMEM = pltpu.MemorySpace.SMEM
KV = KVH * HD
HALF = HD // 2


def pin(array):
    return pltpu.with_memory_space_constraint(array, VMEM)


def rope_tables(position):
    freqs = jnp.exp(jnp.arange(HALF, dtype=f32) * (-2.0 * math.log(rope_base) / HD))
    angles = position[:, None] * freqs[None, :]
    cosine, sine = jnp.cos(angles), jnp.sin(angles)
    return jnp.concatenate([cosine, cosine], 1), jnp.concatenate([-sine, sine], 1)


def rotate(vectors, cosine, sine):
    return vectors * cosine + pltpu.roll(vectors, HALF, 1) * sine


def pieces(value):
    out = []
    for _ in range(3):
        piece = value.astype(bf16).astype(f32)
        out.append(piece)
        value = value - piece
    return out


def exchange(buffer):
    return lax.all_to_all(buffer, "attn", 0, 0, tiled=True)


def lane_of(shape):
    return lax.broadcasted_iota(jnp.int32, shape, 1)


def project_kernel(device, hs, gain, w_query, w_kv, cosine, sine, send, query, normed, kv_rows):
    n, requests, width = hs.shape
    columns = w_query.shape[1]
    square = jnp.zeros((requests, width), f32)
    for k in range(n):
        values = hs[k].astype(f32)
        square = square + values * values
    scale = lax.rsqrt(jnp.sum(square, axis=1, keepdims=True) / (n * width) + 1e-05)
    product = jnp.zeros((requests, columns), f32)
    for k in range(n):
        part = (hs[k].astype(f32) * scale * gain[k : k + 1, :]).astype(bf16)
        normed[k] = part
        product = product + jnp.dot(
            part, w_query[k * width : (k + 1) * width, :], preferred_element_type=f32
        )
    kv = jnp.dot(normed[device[0]], w_kv[...], preferred_element_type=f32)
    for row in range(2 * KVH):
        half, group = divmod(row, KVH)
        value = kv[:, row * HD : (row + 1) * HD]
        upper = value.astype(bf16).astype(f32)
        start = half * 2 * KVH + group
        kv_rows[pl.ds(start, requests, stride=4 * KVH), :] = upper
        kv_rows[pl.ds(start + KVH, requests, stride=4 * KVH), :] = value - upper
    for c in range(columns // HD):
        turned = rotate(product[:, c * HD : (c + 1) * HD], cosine[...], sine[...])
        query[:, c * HD : (c + 1) * HD] = turned.astype(bf16)
    whole = query[...]
    for j in range(n):
        send[j, :, :columns] = whole
        rows = kv_rows[j * 2 * KVH : (j + 1) * 2 * KVH, :]
        if requests > 2 * KVH:
            rows = jnp.concatenate([rows, jnp.zeros((requests - 2 * KVH, HD), f32)], axis=0)
        send[j, :, columns:] = rows.astype(bf16)


def attend_kernel(
    pair_of, live, got, k_cache, v_cache, cosine, sine, send,
    queries, outs, slot_peak, slot_total, peak, total, mixed, kv_block,
):
    n, requests, wide = got.shape
    columns = wide - HD
    heads = columns // HD
    slots, page = k_cache.shape[:2]
    for h in range(H):
        src, c = divmod(h, heads)
        queries[pl.ds(h, requests, stride=H), :] = got[src, :, c * HD : (c + 1) * HD].astype(f32)
    peak[...] = jnp.full_like(peak, lowest)
    total[...] = jnp.zeros_like(total)
    mixed[...] = jnp.zeros_like(mixed)
    places = lane_of((GH, page))
    for s in range(slots):
        rows = pl.ds(pl.multiple_of(pair_of[s] * GH, GH), GH)
        scores = lax.dot_general(
            queries[rows, :].astype(bf16), k_cache[s], (((1,), (1,)), ((), ())),
            preferred_element_type=f32,
        )
        alive = places < live[s]
        scores = jnp.where(alive, scores * score_scale, lowest)
        top = jnp.max(scores, axis=1, keepdims=True)
        weights = jnp.where(alive, jnp.exp(scores - top), 0.0)
        slot_peak[s] = jnp.broadcast_to(top, (GH, HD))
        slot_total[s] = jnp.broadcast_to(jnp.sum(weights, axis=1, keepdims=True), (GH, HD))
        outs[s] = jnp.dot(weights.astype(bf16), v_cache[s], preferred_element_type=f32)
    for s in range(slots):
        rows = pl.ds(pl.multiple_of(pair_of[s] * GH, GH), GH)
        peak[rows, :] = jnp.maximum(peak[rows, :], slot_peak[s])
    for s in range(slots):
        rows = pl.ds(pl.multiple_of(pair_of[s] * GH, GH), GH)
        factor = jnp.exp(slot_peak[s] - peak[rows, :])
        total[rows, :] = total[rows, :] + factor * slot_total[s]
        mixed[rows, :] = mixed[rows, :] + factor * outs[s]

    kv = jnp.zeros((2 * KVH, HD), f32)
    for src in range(n):
        kv = kv + got[src, : 2 * KVH, columns:].astype(f32)
    kv = kv + pltpu.roll(kv, KVH, 0)
    kv = rotate(kv, cosine[...], sine[...])
    upper = lax.broadcasted_iota(jnp.int32, kv.shape, 0) < KVH
    kv = jnp.where(upper, pltpu.roll(kv, HALF, 1), kv)
    if requests > 2 * KVH:
        kv_block[...] = jnp.zeros_like(kv_block)
    kv_block[: 2 * KVH, :] = kv
    lanes = lane_of((requests, HD))
    for j in range(n):
        block = kv_block[...]
        for c in range(heads):
            rows = pl.ds(j * heads + c, requests, stride=H)
            send[j, :, c * HD : (c + 1) * HD] = mixed[rows, :].astype(bf16)
            for i, piece in enumerate(pieces(peak[rows, :]) + pieces(total[rows, :])):
                block = jnp.where(lanes == i * heads + c, piece, block)
        send[j, :, columns:] = block.astype(bf16)


def output_kernel(group_of, got, query, w_out, send, new_entries, entries, attention):
    n, requests, wide = got.shape
    columns = wide - HD
    heads = columns // HD
    width = send.shape[2]
    lanes = lane_of((requests, HD))
    narrow = lane_of((2 * KVH, HD)) < HALF
    for row in range(n):
        request, half = divmod(row, 2)
        block = got[row, : 2 * KVH, columns:].astype(f32)
        block = jnp.where(narrow, pltpu.roll(block, HALF, 1), pltpu.roll(block, KVH, 0))
        rows = pl.ds(half * KVH * requests + request, KVH, stride=requests)
        entries[rows, :] = block[:KVH]
    for i in range(2 * KVH):
        new_entries[:, i * HD : (i + 1) * HD] = entries[
            i * requests : (i + 1) * requests, :
        ].astype(bf16)

    def own(c, half):
        start = (group_of[c] + half * KVH) * requests
        return entries[pl.ds(pl.multiple_of(start, 8), requests), :]

    new_score = jnp.full((requests, HD), lowest, f32)
    for c in range(heads):
        score = query[:, c * HD : (c + 1) * HD].astype(f32) * own(c, 0)
        score = jnp.sum(score, axis=1, keepdims=True) * score_scale
        new_score = jnp.where(lanes == c, score, new_score)
    peaks, totals = [], []
    for src in range(n):
        stats = got[src, :, columns:].astype(f32)
        stats = (
            stats + pltpu.roll(stats, HD - heads, 1) + pltpu.roll(stats, HD - 2 * heads, 1)
        )
        peaks.append(stats)
        totals.append(pltpu.roll(stats, HD - 3 * heads, 1))
    top = new_score
    for value in peaks:
        top = jnp.maximum(top, value)
    weights = [jnp.exp(value - top) for value in peaks]
    new_weight = jnp.exp(new_score - top)
    total = new_weight
    for weight, value in zip(weights, totals):
        total = total + weight * value
    inverse = 1.0 / total
    weights = [weight * inverse for weight in weights]
    new_weight = new_weight * inverse
    for c in range(heads):
        mixed = new_weight[:, c : c + 1] * own(c, 1)
        for src in range(n):
            mixed = mixed + weights[src][:, c : c + 1] * got[
                src, :, c * HD : (c + 1) * HD
            ].astype(f32)
        attention[:, c * HD : (c + 1) * HD] = mixed.astype(bf16)
    whole = attention[...]
    for j in range(n):
        send[j] = jnp.dot(
            whole, w_out[:, j * width : (j + 1) * width], preferred_element_type=f32
        ).astype(bf16)


def call(kernel, out_shape, in_spaces, scratch, limit):
    out_count = len(out_shape)
    return pl.pallas_call(
        kernel,
        out_shape=out_shape,
        in_specs=[pl.BlockSpec(memory_space=space) for space in in_spaces],
        out_specs=[pl.BlockSpec(memory_space=VMEM)] * out_count,
        scratch_shapes=scratch,
        compiler_params=pltpu.CompilerParams(vmem_limit_bytes=limit << 20),
    )


def local(hidden, gain, w_query, w_kv, w_out, k_cache, v_cache, block_table, lengths):
    device = lax.axis_index("attn")
    n = lax.axis_size("attn")
    requests, width = hidden.shape
    columns = w_query.shape[1]
    heads = columns // HD
    slots, page = k_cache.shape[:2]
    pages = block_table.shape[2]
    pairs = requests * KVH
    assert 2 * requests == n

    hs = exchange(jnp.broadcast_to(hidden[None], (n, requests, width)))
    cosine, sine = rope_tables((lengths - 1).astype(f32))
    keys_here = device % 2 == 0
    own_cosine = jnp.where(keys_here, lax.dynamic_slice_in_dim(cosine, device // 2, 1), 1.0)
    own_sine = jnp.where(keys_here, lax.dynamic_slice_in_dim(sine, device // 2, 1), 0.0)
    slot_ids = device * slots + jnp.arange(slots, dtype=jnp.int32)
    matches = block_table.reshape(-1)[None, :] == slot_ids[:, None]
    length_of = jnp.broadcast_to(lengths[:, None, None], block_table.shape).reshape(-1)
    index = jnp.arange(pairs * pages, dtype=jnp.int32)
    live_of = length_of - 1 - index % pages * page
    live = jnp.sum(jnp.where(matches, live_of[None, :], 0), axis=1)
    pair_of = jnp.sum(jnp.where(matches, index[None, :] // pages, 0), axis=1)
    group_of = (device * heads + jnp.arange(heads, dtype=jnp.int32)) // GH

    wide = jax.ShapeDtypeStruct((n, requests, columns + HD), bf16)
    send, query = call(
        project_kernel,
        [wide, jax.ShapeDtypeStruct((requests, columns), bf16)],
        [SMEM] + [VMEM] * 6,
        [pltpu.VMEM(hs.shape, bf16), pltpu.VMEM((n * 2 * KVH, HD), f32)],
        6,
    )(device.reshape(1), hs, gain.reshape(n, width), pin(w_query), pin(w_kv), cosine, sine)
    got = exchange(send)
    stat = pltpu.VMEM((pairs * GH, HD), f32)
    slot_stat = pltpu.VMEM((slots, GH, HD), f32)
    (send,) = call(
        attend_kernel,
        [wide],
        [SMEM] * 2 + [VMEM] * 5,
        [stat] + [slot_stat] * 3 + [stat] * 3 + [pltpu.VMEM((requests, HD), f32)],
        8,
    )(pair_of, live, got, pin(k_cache), pin(v_cache), own_cosine, own_sine)
    got = exchange(send)
    send, new_entries = call(
        output_kernel,
        [
            jax.ShapeDtypeStruct((n, requests, width), bf16),
            jax.ShapeDtypeStruct((requests, 2 * KV), bf16),
        ],
        [SMEM] + [VMEM] * 3,
        [pltpu.VMEM((2 * KVH * requests, HD), f32), pltpu.VMEM((requests, columns), bf16)],
        6,
    )(group_of, got, query, pin(w_out))
    got = exchange(send)
    attn_out = jnp.sum(got.astype(f32), axis=0).astype(bf16)
    return attn_out, new_entries


def solution(mesh):
    in_specs = (
        P("groups", "attn"),
        P(),
        P(None, "attn"),
        P("attn", None),
        P("attn", None),
        P(("groups", "attn"), None, None),
        P(("groups", "attn"), None, None),
        P("groups", None, None),
        P("groups"),
    )
    out_specs = (P("groups", "attn"), P("groups", None))
    return jax.shard_map(local, mesh=mesh, in_specs=in_specs, out_specs=out_specs, check_vma=False)
```

```python
import functools
import math

import jax
import jax.numpy as jnp
from jax import lax
from jax.experimental import pallas as pl
from jax.experimental.pallas import tpu as pltpu
from jax.sharding import PartitionSpec as P

HD = 128
H = 64
KVH = 4
GH = H // KVH

lowest = -1e30
rope_base = 500000.0
score_scale = 1.0 / math.sqrt(HD)
bf16 = jnp.bfloat16
f32 = jnp.float32
VMEM = pltpu.MemorySpace.VMEM
SMEM = pltpu.MemorySpace.SMEM
KV = KVH * HD
PAGE = 128
HALF = HD // 2


def rotate(vectors, cosine, sine):
    return vectors * cosine + pltpu.roll(vectors, HALF, 1) * sine


def exchange(buffer):
    return lax.all_to_all(buffer, "attn", 0, 0, tiled=True)


def lane_of(shape):
    return lax.broadcasted_iota(jnp.int32, shape, 1)


def spread_kernel(device, hidden, send):
    for j in range(send.shape[0]):
        send[j] = hidden[...]


def add_kernel(got, out):
    total = got[0].astype(f32)
    for src in range(1, got.shape[0]):
        total = total + got[src].astype(f32)
    out[...] = total.astype(bf16)


def place_slots(device, lengths, table, pair_of, live, slots, total):
    requests = table.shape[0]
    slot = device * slots + lane_of((1, HD))
    pair = jnp.full((1, HD), requests * KVH, jnp.int32)
    alive = jnp.zeros((1, HD), jnp.int32)
    for r in range(requests):
        pages = lax.div(lengths[r] + PAGE - 1, PAGE)
        offset = slot - table[r, 0, 0]
        offset = jnp.where(offset < 0, offset + total, offset)
        here = offset < KVH * pages
        group = jnp.zeros((1, HD), jnp.int32)
        for g in range(1, KVH):
            group = group + (offset >= g * pages).astype(jnp.int32)
        pair = jnp.where(here, r * KVH + group, pair)
        alive = jnp.where(here, lengths[r] - 1 - (offset - group * pages) * PAGE, alive)
    pair_of[...] = pair
    live[...] = alive


def project_kernel(
    device, lengths, table, hs, gain, w_query, w_kv,
    send, query, own_tables, pair_of, live, normed, kv_rows, tables, *, slots,
):
    n, requests, width = hs.shape
    columns = w_query.shape[1]
    square = jnp.zeros((requests, width), f32)
    for k in range(n):
        values = hs[k].astype(f32)
        square = square + values * values
    scale = lax.rsqrt(jnp.sum(square, axis=1, keepdims=True) / (n * width) + 1e-05)

    row, lane = lax.broadcasted_iota(jnp.int32, (requests, HD), 0), lane_of((requests, HD))
    position = jnp.zeros((requests, HD), f32)
    for r in range(requests):
        position = jnp.where(row == r, (lengths[r] - 1).astype(f32), position)
    index = jnp.where(lane < HALF, lane, lane - HALF).astype(f32)
    angles = position * jnp.exp(index * (-2.0 * math.log(rope_base) / HD))
    cosine = jnp.cos(angles)
    sine = jnp.sin(angles)
    sine = jnp.where(lane < HALF, -sine, sine)
    tables[:requests] = cosine
    tables[requests:] = sine
    mine = lax.div(device[0], 2)
    keys_here = lax.rem(device[0], 2) == 0
    own_tables[0:1, :] = jnp.where(keys_here, tables[pl.ds(mine, 1), :], 1.0)
    own_tables[1:2, :] = jnp.where(keys_here, tables[pl.ds(requests + mine, 1), :], 0.0)
    place_slots(device[0], lengths, table, pair_of, live, slots, n * slots)

    product = jnp.zeros((requests, columns), f32)
    for k in range(n):
        part = hs[k].astype(f32) * scale * gain[:, k * width : (k + 1) * width]
        part = part.astype(bf16)
        normed[k] = part
        product = product + jnp.dot(
            part, w_query[k * width : (k + 1) * width, :], preferred_element_type=f32
        )
    kv = jnp.dot(normed[device[0]], w_kv[...], preferred_element_type=f32)
    for i in range(2 * KVH):
        half, group = divmod(i, KVH)
        value = kv[:, i * HD : (i + 1) * HD]
        upper = value.astype(bf16).astype(f32)
        start = half * 2 * KVH + group
        kv_rows[pl.ds(start, requests, stride=4 * KVH), :] = upper
        kv_rows[pl.ds(start + KVH, requests, stride=4 * KVH), :] = value - upper
    for c in range(columns // HD):
        turned = rotate(product[:, c * HD : (c + 1) * HD], cosine, sine)
        query[:, c * HD : (c + 1) * HD] = turned.astype(bf16)
    whole = query[...]
    for j in range(n):
        send[j, :, :columns] = whole
        rows = kv_rows[j * 2 * KVH : (j + 1) * 2 * KVH, :]
        if requests > 2 * KVH:
            rows = jnp.concatenate([rows, jnp.zeros((requests - 2 * KVH, HD), f32)], axis=0)
        send[j, :, columns:] = rows.astype(bf16)


def attend_kernel(
    pair_of, live, got, k_cache, v_cache, own_tables, send,
    queries, slot_score, slot_weight, slot_out, slot_peak, slot_total, peak, total, mixed, kv_block,
):
    n, requests, wide = got.shape
    columns = wide - HD
    heads = columns // HD
    slots, page = k_cache.shape[:2]
    for h in range(H):
        src, c = divmod(h, heads)
        queries[pl.ds(h, requests, stride=H), :] = got[src, :, c * HD : (c + 1) * HD].astype(f32)
    queries[requests * H :, :] = jnp.zeros((GH, HD), f32)
    peak[...] = jnp.full_like(peak, lowest)
    total[...] = jnp.zeros_like(total)
    mixed[...] = jnp.zeros_like(mixed)

    def rows_of(s):
        return pl.ds(pl.multiple_of(pair_of[0, s] * GH, GH), GH)

    for s in range(slots):
        slot_score[s] = lax.dot_general(
            queries[rows_of(s), :].astype(bf16), k_cache[s], (((1,), (1,)), ((), ())),
            preferred_element_type=f32,
        )
    places = lane_of((GH, page))
    for s in range(slots):
        alive = places < live[0, s]
        scores = jnp.where(alive, slot_score[s] * score_scale, lowest)
        top = jnp.max(scores, axis=1, keepdims=True)
        weights = jnp.where(alive, jnp.exp(scores - top), 0.0)
        slot_weight[s] = weights.astype(bf16)
        slot_peak[s] = jnp.broadcast_to(top, (GH, HD))
        slot_total[s] = jnp.broadcast_to(jnp.sum(weights, axis=1, keepdims=True), (GH, HD))
    for s in range(slots):
        slot_out[s] = jnp.dot(slot_weight[s], v_cache[s], preferred_element_type=f32)
    running = slot_peak[0]
    peak[rows_of(0), :] = running
    for s in range(1, slots):
        value = slot_peak[s]
        same = pair_of[0, s] == pair_of[0, s - 1]
        running = jnp.maximum(value, jnp.where(same, running, lowest))
        peak[rows_of(s), :] = running
    run_total = jnp.zeros((GH, HD), f32)
    run_mixed = jnp.zeros((GH, HD), f32)
    for s in range(slots):
        factor = jnp.exp(slot_peak[s] - peak[rows_of(s), :])
        keep = jnp.where(pair_of[0, s] == pair_of[0, max(s - 1, 0)], 1.0, 0.0)
        run_total = keep * run_total + factor * slot_total[s]
        run_mixed = keep * run_mixed + factor * slot_out[s]
        total[rows_of(s), :] = run_total
        mixed[rows_of(s), :] = run_mixed

    kv = jnp.zeros((2 * KVH, HD), f32)
    for src in range(n):
        kv = kv + got[src, : 2 * KVH, columns:].astype(f32)
    kv = kv + pltpu.roll(kv, KVH, 0)
    kv = rotate(kv, own_tables[0:1, :], own_tables[1:2, :])
    upper = lax.broadcasted_iota(jnp.int32, kv.shape, 0) < KVH
    kv = jnp.where(upper, pltpu.roll(kv, HALF, 1), kv)
    if requests > 2 * KVH:
        kv_block[...] = jnp.zeros_like(kv_block)
    kv_block[: 2 * KVH, :] = kv
    lanes = lane_of((requests, HD))
    order = lax.rem(lanes, heads)
    kind = lax.div(lanes, heads)
    for j in range(n):
        stats = jnp.zeros((requests, HD), f32)
        for c in range(heads):
            rows = pl.ds(j * heads + c, requests, stride=H)
            send[j, :, c * HD : (c + 1) * HD] = mixed[rows, :].astype(bf16)
            value = jnp.where(kind < 3, peak[rows, :], total[rows, :])
            stats = jnp.where(order == c, value, stats)
        first = stats.astype(bf16).astype(f32)
        stats = stats - first
        second = stats.astype(bf16).astype(f32)
        third = stats - second
        kinds = lax.rem(kind, 3)
        stats = jnp.where(kinds == 0, first, jnp.where(kinds == 1, second, third))
        send[j, :, columns:] = jnp.where(kind < 6, stats, kv_block[...]).astype(bf16)


def output_kernel(device, got, query, w_out, send, new_entries, entries, attention):
    n, requests, wide = got.shape
    columns = wide - HD
    heads = columns // HD
    width = send.shape[2]
    lanes = lane_of((requests, HD))
    narrow = lane_of((2 * KVH, HD)) < HALF
    for row in range(n):
        request, half = divmod(row, 2)
        block = got[row, : 2 * KVH, columns:].astype(f32)
        block = jnp.where(narrow, pltpu.roll(block, HALF, 1), pltpu.roll(block, KVH, 0))
        rows = pl.ds(half * KVH * requests + request, KVH, stride=requests)
        entries[rows, :] = block[:KVH]
    for i in range(2 * KVH):
        new_entries[:, i * HD : (i + 1) * HD] = entries[
            i * requests : (i + 1) * requests, :
        ].astype(bf16)

    def own(c, half):
        start = (lax.div(device[0] * heads + c, GH) + half * KVH) * requests
        return entries[pl.ds(pl.multiple_of(start, 8), requests), :]

    new_score = jnp.full((requests, HD), lowest, f32)
    for c in range(heads):
        score = query[:, c * HD : (c + 1) * HD].astype(f32) * own(c, 0)
        score = jnp.sum(score, axis=1, keepdims=True) * score_scale
        new_score = jnp.where(lanes == c, score, new_score)
    peaks, totals = [], []
    for src in range(n):
        stats = got[src, :, columns:].astype(f32)
        stats = (
            stats + pltpu.roll(stats, HD - heads, 1) + pltpu.roll(stats, HD - 2 * heads, 1)
        )
        peaks.append(stats)
        totals.append(pltpu.roll(stats, HD - 3 * heads, 1))
    top = new_score
    for value in peaks:
        top = jnp.maximum(top, value)
    weights = [jnp.exp(value - top) for value in peaks]
    new_weight = jnp.exp(new_score - top)
    total = new_weight
    for weight, value in zip(weights, totals):
        total = total + weight * value
    inverse = 1.0 / total
    weights = [weight * inverse for weight in weights]
    new_weight = new_weight * inverse
    for c in range(heads):
        mixed = new_weight[:, c : c + 1] * own(c, 1)
        for src in range(n):
            mixed = mixed + weights[src][:, c : c + 1] * got[
                src, :, c * HD : (c + 1) * HD
            ].astype(f32)
        attention[:, c * HD : (c + 1) * HD] = mixed.astype(bf16)
    whole = attention[...]
    for j in range(n):
        send[j] = jnp.dot(
            whole, w_out[:, j * width : (j + 1) * width], preferred_element_type=f32
        ).astype(bf16)


def call(kernel, out_shape, in_spaces, out_spaces, scratch, limit, moved=None):
    return pl.pallas_call(
        kernel,
        out_shape=out_shape,
        in_specs=[pl.BlockSpec(memory_space=space) for space in in_spaces],
        out_specs=[pl.BlockSpec(memory_space=space) for space in out_spaces],
        scratch_shapes=scratch,
        compiler_params=pltpu.CompilerParams(vmem_limit_bytes=limit << 20),
        cost_estimate=moved
        and pl.CostEstimate(flops=moved * 512, bytes_accessed=moved, transcendentals=0),
    )


def local(hidden, gain, w_query, w_kv, w_out, k_cache, v_cache, block_table, lengths):
    device = lax.axis_index("attn").astype(jnp.int32).reshape(1)
    n = lax.axis_size("attn")
    requests, width = hidden.shape
    columns = w_query.shape[1]
    slots = k_cache.shape[0]
    pairs = requests * KVH
    assert 2 * requests == n

    shape = jax.ShapeDtypeStruct
    (send,) = call(
        spread_kernel,
        [shape((n, requests, width), bf16)],
        [SMEM, VMEM],
        [VMEM],
        [],
        2,
        2 * (w_query.nbytes + w_kv.nbytes),
    )(device, hidden)
    hs = exchange(send)
    wide = shape((n, requests, columns + HD), bf16)
    send, query, own_tables, pair_of, live = call(
        functools.partial(project_kernel, slots=slots),
        [
            wide,
            shape((requests, columns), bf16),
            shape((2, HD), f32),
            shape((1, HD), jnp.int32),
            shape((1, HD), jnp.int32),
        ],
        [SMEM] * 3 + [VMEM] * 4,
        [VMEM] * 5,
        [
            pltpu.VMEM(hs.shape, bf16),
            pltpu.VMEM((n * 2 * KVH, HD), f32),
            pltpu.VMEM((2 * requests, HD), f32),
        ],
        4,
    )(device, lengths, block_table, hs, gain.reshape(1, n * width), w_query, w_kv)
    got = exchange(send)
    rows = pltpu.VMEM(((pairs + 1) * GH, HD), f32)
    slot_rows = pltpu.VMEM((slots, GH, HD), f32)
    (send,) = call(
        attend_kernel,
        [wide],
        [SMEM] * 2 + [VMEM] * 4,
        [VMEM],
        [rows, slot_rows, pltpu.VMEM((slots, GH, HD), bf16)]
        + [slot_rows] * 3
        + [rows] * 3
        + [pltpu.VMEM((requests, HD), f32)],
        8,
    )(pair_of, live, got, k_cache, v_cache, own_tables)
    got = exchange(send)
    send, new_entries = call(
        output_kernel,
        [shape((n, requests, width), bf16), shape((requests, 2 * KV), bf16)],
        [SMEM] + [VMEM] * 3,
        [VMEM] * 2,
        [pltpu.VMEM((2 * KVH * requests, HD), f32), pltpu.VMEM((requests, columns), bf16)],
        4,
    )(device, got, query, w_out)
    got = exchange(send)
    (attn_out,) = call(add_kernel, [shape((requests, width), bf16)], [VMEM], [VMEM], [], 4)(got)
    return attn_out, new_entries


def solution(mesh):
    in_specs = (
        P("groups", "attn"),
        P(),
        P(None, "attn"),
        P("attn", None),
        P("attn", None),
        P(("groups", "attn"), None, None),
        P(("groups", "attn"), None, None),
        P("groups", None, None),
        P("groups"),
    )
    out_specs = (P("groups", "attn"), P("groups", None))
    return jax.shard_map(local, mesh=mesh, in_specs=in_specs, out_specs=out_specs, check_vma=False)
```

```python
import functools
import math

import jax
import jax.numpy as jnp
from jax import lax
from jax.experimental import pallas as pl
from jax.experimental.pallas import tpu as pltpu
from jax.sharding import PartitionSpec as P

HD = 128
H = 64
KVH = 4
GH = H // KVH

lowest = -1e30
rope_base = 500000.0
score_scale = 1.0 / math.sqrt(HD)
bf16 = jnp.bfloat16
f32 = jnp.float32
VMEM = pltpu.MemorySpace.VMEM
SMEM = pltpu.MemorySpace.SMEM
KV = KVH * HD
PAGE = 128
HALF = HD // 2


def rotate(vectors, cosine, sine):
    return vectors * cosine + pltpu.roll(vectors, HALF, 1) * sine


def exchange(buffer):
    return lax.all_to_all(buffer, "attn", 0, 0, tiled=True)


def exchange_same_core(buffer):
    chips = buffer.shape[0]
    groups = [[2 * chip + core for chip in range(chips)] for core in range(2)]
    return lax.all_to_all(buffer, "attn", 0, 0, tiled=True, axis_index_groups=groups)


def swap_cores(buffer):
    n = lax.axis_size("attn")
    return lax.ppermute(buffer, "attn", [(i, i ^ 1) for i in range(n)])


def lane_of(shape):
    return lax.broadcasted_iota(jnp.int32, shape, 1)


def spread_kernel(device, hidden, send):
    for j in range(send.shape[0]):
        send[j] = hidden[...]


def add_kernel(got, out):
    total = got[0].astype(f32)
    for src in range(1, got.shape[0]):
        total = total + got[src].astype(f32)
    out[...] = total.astype(bf16)


def place_slots(device, lengths, table, pair_of, live, slots, total):
    requests = table.shape[0]
    slot = device * slots + lane_of((1, HD))
    pair = jnp.full((1, HD), requests * KVH, jnp.int32)
    alive = jnp.zeros((1, HD), jnp.int32)
    for r in range(requests):
        pages = lax.div(lengths[r] + PAGE - 1, PAGE)
        offset = slot - table[r, 0, 0]
        offset = jnp.where(offset < 0, offset + total, offset)
        here = offset < KVH * pages
        group = jnp.zeros((1, HD), jnp.int32)
        for g in range(1, KVH):
            group = group + (offset >= g * pages).astype(jnp.int32)
        pair = jnp.where(here, r * KVH + group, pair)
        alive = jnp.where(here, lengths[r] - 1 - (offset - group * pages) * PAGE, alive)
    pair_of[...] = pair
    live[...] = alive


def prepare_kernel(
    device, lengths, table, near, tables, own_tables, pair_of, live, square, *, slots
):
    chips, requests, _ = near.shape
    total = jnp.zeros(square.shape, f32)
    for chip in range(chips):
        values = near[chip].astype(f32)
        total = total + values * values
    square[...] = total
    row, lane = lax.broadcasted_iota(jnp.int32, (requests, HD), 0), lane_of((requests, HD))
    position = jnp.zeros((requests, HD), f32)
    for r in range(requests):
        position = jnp.where(row == r, (lengths[r] - 1).astype(f32), position)
    index = jnp.where(lane < HALF, lane, lane - HALF).astype(f32)
    angles = position * jnp.exp(index * (-2.0 * math.log(rope_base) / HD))
    sine = jnp.sin(angles)
    tables[:requests] = jnp.cos(angles)
    tables[requests:] = jnp.where(lane < HALF, -sine, sine)
    mine = lax.div(device[0], 2)
    keys_here = lax.rem(device[0], 2) == 0
    own_tables[0:1, :] = jnp.where(keys_here, tables[pl.ds(mine, 1), :], 1.0)
    own_tables[1:2, :] = jnp.where(keys_here, tables[pl.ds(requests + mine, 1), :], 0.0)
    place_slots(device[0], lengths, table, pair_of, live, slots, 2 * chips * slots)


def project_kernel(
    device, near, far, square, tables, gain, w_query, w_kv, send, query, kv_rows
):
    chips, requests, width = near.shape
    n = 2 * chips
    columns = w_query.shape[1]
    core = lax.rem(device[0], 2)
    total = square[...]
    for chip in range(chips):
        values = far[chip].astype(f32)
        total = total + values * values
    scale = lax.rsqrt(jnp.sum(total, axis=1, keepdims=True) / (n * width) + 1e-05)
    product = jnp.zeros((requests, columns), f32)
    for k in range(n):
        chip, from_core = divmod(k, 2)
        values = jnp.where(core == from_core, near[chip].astype(f32), far[chip].astype(f32))
        part = (values * scale * gain[:, k * width : (k + 1) * width]).astype(bf16)
        product = product + jnp.dot(
            part, w_query[k * width : (k + 1) * width, :], preferred_element_type=f32
        )
    own_gain = gain[:, pl.ds(pl.multiple_of(device[0] * width, HD), width)]
    own = (near[lax.div(device[0], 2)].astype(f32) * scale * own_gain).astype(bf16)
    kv = jnp.dot(own, w_kv[...], preferred_element_type=f32)
    cosine, sine = tables[:requests], tables[requests:]
    for i in range(2 * KVH):
        half, group = divmod(i, KVH)
        value = kv[:, i * HD : (i + 1) * HD]
        upper = value.astype(bf16).astype(f32)
        start = half * 2 * KVH + group
        kv_rows[pl.ds(start, requests, stride=4 * KVH), :] = upper
        kv_rows[pl.ds(start + KVH, requests, stride=4 * KVH), :] = value - upper
    for c in range(columns // HD):
        turned = rotate(product[:, c * HD : (c + 1) * HD], cosine, sine)
        query[:, c * HD : (c + 1) * HD] = turned.astype(bf16)
    whole = query[...]
    for j in range(n):
        send[j, :, :columns] = whole
        rows = kv_rows[j * 2 * KVH : (j + 1) * 2 * KVH, :]
        if requests > 2 * KVH:
            rows = jnp.concatenate([rows, jnp.zeros((requests - 2 * KVH, HD), f32)], axis=0)
        send[j, :, columns:] = rows.astype(bf16)


def attend_kernel(
    pair_of, live, got, k_cache, v_cache, own_tables, send,
    queries, slot_score, slot_weight, slot_out, slot_peak, slot_total, peak, total, mixed, kv_block,
):
    n, requests, wide = got.shape
    columns = wide - HD
    heads = columns // HD
    slots, page = k_cache.shape[:2]
    for h in range(H):
        src, c = divmod(h, heads)
        queries[pl.ds(h, requests, stride=H), :] = got[src, :, c * HD : (c + 1) * HD].astype(f32)
    queries[requests * H :, :] = jnp.zeros((GH, HD), f32)
    peak[...] = jnp.full_like(peak, lowest)
    total[...] = jnp.zeros_like(total)
    mixed[...] = jnp.zeros_like(mixed)

    def rows_of(s):
        return pl.ds(pl.multiple_of(pair_of[0, s] * GH, GH), GH)

    for s in range(slots):
        slot_score[s] = lax.dot_general(
            queries[rows_of(s), :].astype(bf16), k_cache[s], (((1,), (1,)), ((), ())),
            preferred_element_type=f32,
        )
    places = lane_of((GH, page))
    for s in range(slots):
        alive = places < live[0, s]
        scores = jnp.where(alive, slot_score[s] * score_scale, lowest)
        top = jnp.max(scores, axis=1, keepdims=True)
        weights = jnp.where(alive, jnp.exp(scores - top), 0.0)
        slot_weight[s] = weights.astype(bf16)
        slot_peak[s] = jnp.broadcast_to(top, (GH, HD))
        slot_total[s] = jnp.broadcast_to(jnp.sum(weights, axis=1, keepdims=True), (GH, HD))
    for s in range(slots):
        slot_out[s] = jnp.dot(slot_weight[s], v_cache[s], preferred_element_type=f32)
    running = slot_peak[0]
    peak[rows_of(0), :] = running
    for s in range(1, slots):
        value = slot_peak[s]
        same = pair_of[0, s] == pair_of[0, s - 1]
        running = jnp.maximum(value, jnp.where(same, running, lowest))
        peak[rows_of(s), :] = running
    run_total = jnp.zeros((GH, HD), f32)
    run_mixed = jnp.zeros((GH, HD), f32)
    for s in range(slots):
        factor = jnp.exp(slot_peak[s] - peak[rows_of(s), :])
        keep = jnp.where(pair_of[0, s] == pair_of[0, max(s - 1, 0)], 1.0, 0.0)
        run_total = keep * run_total + factor * slot_total[s]
        run_mixed = keep * run_mixed + factor * slot_out[s]
        total[rows_of(s), :] = run_total
        mixed[rows_of(s), :] = run_mixed

    kv = jnp.zeros((2 * KVH, HD), f32)
    for src in range(n):
        kv = kv + got[src, : 2 * KVH, columns:].astype(f32)
    kv = kv + pltpu.roll(kv, KVH, 0)
    kv = rotate(kv, own_tables[0:1, :], own_tables[1:2, :])
    upper = lax.broadcasted_iota(jnp.int32, kv.shape, 0) < KVH
    kv = jnp.where(upper, pltpu.roll(kv, HALF, 1), kv)
    if requests > 2 * KVH:
        kv_block[...] = jnp.zeros_like(kv_block)
    kv_block[: 2 * KVH, :] = kv
    lanes = lane_of((requests, HD))
    order = lax.rem(lanes, heads)
    kind = lax.div(lanes, heads)
    for j in range(n):
        stats = jnp.zeros((requests, HD), f32)
        for c in range(heads):
            rows = pl.ds(j * heads + c, requests, stride=H)
            send[j, :, c * HD : (c + 1) * HD] = mixed[rows, :].astype(bf16)
            value = jnp.where(kind < 3, peak[rows, :], total[rows, :])
            stats = jnp.where(order == c, value, stats)
        first = stats.astype(bf16).astype(f32)
        stats = stats - first
        second = stats.astype(bf16).astype(f32)
        third = stats - second
        kinds = lax.rem(kind, 3)
        stats = jnp.where(kinds == 0, first, jnp.where(kinds == 1, second, third))
        send[j, :, columns:] = jnp.where(kind < 6, stats, kv_block[...]).astype(bf16)


def multiply_out(attention, w_out, result, core):
    chips, _, width = result.shape
    whole = attention[...]
    for chip in range(chips):
        columns = pl.ds(pl.multiple_of((2 * chip + core) * width, HD), width)
        result[chip] = jnp.dot(
            whole, w_out[:, columns], preferred_element_type=f32
        ).astype(result.dtype)


def combine_kernel(device, got, query, w_out, away, new_entries, attention, entries):
    n, requests, wide = got.shape
    columns = wide - HD
    heads = columns // HD
    lanes = lane_of((requests, HD))
    narrow = lane_of((2 * KVH, HD)) < HALF
    for row in range(n):
        request, half = divmod(row, 2)
        block = got[row, : 2 * KVH, columns:].astype(f32)
        block = jnp.where(narrow, pltpu.roll(block, HALF, 1), pltpu.roll(block, KVH, 0))
        rows = pl.ds(half * KVH * requests + request, KVH, stride=requests)
        entries[rows, :] = block[:KVH]
    for i in range(2 * KVH):
        new_entries[:, i * HD : (i + 1) * HD] = entries[
            i * requests : (i + 1) * requests, :
        ].astype(bf16)

    def own(c, half):
        start = (lax.div(device[0] * heads + c, GH) + half * KVH) * requests
        return entries[pl.ds(pl.multiple_of(start, 8), requests), :]

    new_score = jnp.full((requests, HD), lowest, f32)
    for c in range(heads):
        score = query[:, c * HD : (c + 1) * HD].astype(f32) * own(c, 0)
        score = jnp.sum(score, axis=1, keepdims=True) * score_scale
        new_score = jnp.where(lanes == c, score, new_score)
    peaks, totals = [], []
    for src in range(n):
        stats = got[src, :, columns:].astype(f32)
        stats = (
            stats + pltpu.roll(stats, HD - heads, 1) + pltpu.roll(stats, HD - 2 * heads, 1)
        )
        peaks.append(stats)
        totals.append(pltpu.roll(stats, HD - 3 * heads, 1))
    top = new_score
    for value in peaks:
        top = jnp.maximum(top, value)
    weights = [jnp.exp(value - top) for value in peaks]
    new_weight = jnp.exp(new_score - top)
    total = new_weight
    for weight, value in zip(weights, totals):
        total = total + weight * value
    inverse = 1.0 / total
    weights = [weight * inverse for weight in weights]
    new_weight = new_weight * inverse
    for c in range(heads):
        mixed = new_weight[:, c : c + 1] * own(c, 1)
        for src in range(n):
            mixed = mixed + weights[src][:, c : c + 1] * got[
                src, :, c * HD : (c + 1) * HD
            ].astype(f32)
        attention[:, c * HD : (c + 1) * HD] = mixed.astype(bf16)
    multiply_out(attention, w_out, away, 1 - lax.rem(device[0], 2))


def keep_kernel(device, attention, w_out, kept):
    multiply_out(attention, w_out, kept, lax.rem(device[0], 2))


def join_kernel(kept, came, send):
    for chip in range(send.shape[0]):
        send[chip] = (kept[chip] + came[chip].astype(f32)).astype(bf16)


def call(kernel, out_shape, in_spaces, out_spaces, scratch, limit, moved=None):
    return pl.pallas_call(
        kernel,
        out_shape=out_shape,
        in_specs=[pl.BlockSpec(memory_space=space) for space in in_spaces],
        out_specs=[pl.BlockSpec(memory_space=space) for space in out_spaces],
        scratch_shapes=scratch,
        compiler_params=pltpu.CompilerParams(vmem_limit_bytes=limit << 20),
        cost_estimate=moved
        and pl.CostEstimate(flops=moved * 512, bytes_accessed=moved, transcendentals=0),
    )


def local(hidden, gain, w_query, w_kv, w_out, k_cache, v_cache, block_table, lengths):
    device = lax.axis_index("attn").astype(jnp.int32).reshape(1)
    n = lax.axis_size("attn")
    requests, width = hidden.shape
    columns = w_query.shape[1]
    slots = k_cache.shape[0]
    pairs = requests * KVH
    assert 2 * requests == n

    shape = jax.ShapeDtypeStruct
    halves = shape((n // 2, requests, width), bf16)
    wide = shape((n, requests, columns + HD), bf16)
    (send,) = call(
        spread_kernel,
        [halves],
        [SMEM, VMEM],
        [VMEM],
        [],
        2,
        2 * (w_query.nbytes + w_kv.nbytes),
    )(device, hidden)
    near = exchange_same_core(send)
    far = swap_cores(near)
    tables, own_tables, pair_of, live, square = call(
        functools.partial(prepare_kernel, slots=slots),
        [
            shape((2 * requests, HD), f32),
            shape((2, HD), f32),
            shape((1, HD), jnp.int32),
            shape((1, HD), jnp.int32),
            shape((requests, width), f32),
        ],
        [SMEM] * 3 + [VMEM],
        [VMEM] * 5,
        [],
        2,
    )(device, lengths, block_table, near)
    send, query = call(
        project_kernel,
        [wide, shape((requests, columns), bf16)],
        [SMEM] + [VMEM] * 7,
        [VMEM] * 2,
        [pltpu.VMEM((n * 2 * KVH, HD), f32)],
        4,
    )(device, near, far, square, tables, gain.reshape(1, n * width), w_query, w_kv)
    got = exchange(send)
    rows = pltpu.VMEM(((pairs + 1) * GH, HD), f32)
    slot_rows = pltpu.VMEM((slots, GH, HD), f32)
    (send,) = call(
        attend_kernel,
        [wide],
        [SMEM] * 2 + [VMEM] * 4,
        [VMEM],
        [rows, slot_rows, pltpu.VMEM((slots, GH, HD), bf16)]
        + [slot_rows] * 3
        + [rows] * 3
        + [pltpu.VMEM((requests, HD), f32)],
        8,
    )(pair_of, live, got, k_cache, v_cache, own_tables)
    got = exchange(send)
    away, new_entries, attention = call(
        combine_kernel,
        [halves, shape((requests, 2 * KV), bf16), shape((requests, columns), bf16)],
        [SMEM] + [VMEM] * 3,
        [VMEM] * 3,
        [pltpu.VMEM((2 * KVH * requests, HD), f32)],
        4,
    )(device, got, query, w_out)
    came = swap_cores(away)
    (kept,) = call(
        keep_kernel, [shape(halves.shape, f32)], [SMEM] + [VMEM] * 2, [VMEM], [], 4
    )(device, attention, w_out)
    (send,) = call(join_kernel, [halves], [VMEM] * 2, [VMEM], [], 4)(kept, came)
    got = exchange_same_core(send)
    (attn_out,) = call(add_kernel, [shape((requests, width), bf16)], [VMEM], [VMEM], [], 4)(got)
    return attn_out, new_entries


def solution(mesh):
    in_specs = (
        P("groups", "attn"),
        P(),
        P(None, "attn"),
        P("attn", None),
        P("attn", None),
        P(("groups", "attn"), None, None),
        P(("groups", "attn"), None, None),
        P("groups", None, None),
        P("groups"),
    )
    out_specs = (P("groups", "attn"), P("groups", None))
    return jax.shard_map(local, mesh=mesh, in_specs=in_specs, out_specs=out_specs, check_vma=False)
```

```python
import functools
import math

import jax
import jax.numpy as jnp
from jax import lax
from jax.experimental import pallas as pl
from jax.experimental.pallas import tpu as pltpu
from jax.sharding import PartitionSpec as P

HD = 128
H = 64
KVH = 4
GH = H // KVH
CORE_H = H // 2
CORE_GH = GH // 2

lowest = -1e30
rope_base = 500000.0
score_scale = 1.0 / math.sqrt(HD)
bf16 = jnp.bfloat16
f32 = jnp.float32
VMEM = pltpu.MemorySpace.VMEM
SMEM = pltpu.MemorySpace.SMEM
KV = KVH * HD
PAGE = 128
HALF = HD // 2


def rotate(vectors, cosine, sine):
    return vectors * cosine + pltpu.roll(vectors, HALF, 1) * sine


def exchange(buffer):
    chips = buffer.shape[0]
    groups = [[2 * chip + core for chip in range(chips)] for core in range(2)]
    return lax.all_to_all(buffer, "attn", 0, 0, tiled=True, axis_index_groups=groups)


def swap_cores(buffer):
    n = lax.axis_size("attn")
    return lax.ppermute(buffer, "attn", [(i, i ^ 1) for i in range(n)])


def lane_of(shape):
    return lax.broadcasted_iota(jnp.int32, shape, 1)


def spread_kernel(device, hidden, send):
    for j in range(send.shape[0]):
        send[j] = hidden[...]


def add_kernel(got, out):
    total = got[0].astype(f32)
    for src in range(1, got.shape[0]):
        total = total + got[src].astype(f32)
    out[...] = total.astype(bf16)


def place_slots(device, lengths, table, pair_of, live, slots, total):
    requests = table.shape[0]
    lane = lane_of((1, HD))
    partner = device + 1 - 2 * lax.rem(device, 2)
    slot = jnp.where(lane < slots, device * slots + lane, (partner - 1) * slots + lane)
    pair = jnp.full((1, HD), requests * KVH, jnp.int32)
    alive = jnp.zeros((1, HD), jnp.int32)
    for r in range(requests):
        pages = lax.div(lengths[r] + PAGE - 1, PAGE)
        offset = slot - table[r, 0, 0]
        offset = jnp.where(offset < 0, offset + total, offset)
        here = offset < KVH * pages
        group = jnp.zeros((1, HD), jnp.int32)
        for g in range(1, KVH):
            group = group + (offset >= g * pages).astype(jnp.int32)
        pair = jnp.where(here, r * KVH + group, pair)
        alive = jnp.where(here, lengths[r] - 1 - (offset - group * pages) * PAGE, alive)
    pair_of[...] = pair
    live[...] = alive


def prepare_kernel(
    device, lengths, table, near, tables, own_tables, pair_of, live, square, *, slots
):
    chips, requests, _ = near.shape
    total = jnp.zeros(square.shape, f32)
    for chip in range(chips):
        values = near[chip].astype(f32)
        total = total + values * values
    square[...] = total
    row, lane = lax.broadcasted_iota(jnp.int32, (requests, HD), 0), lane_of((requests, HD))
    position = jnp.zeros((requests, HD), f32)
    for r in range(requests):
        position = jnp.where(row == r, (lengths[r] - 1).astype(f32), position)
    index = jnp.where(lane < HALF, lane, lane - HALF).astype(f32)
    angles = position * jnp.exp(index * (-2.0 * math.log(rope_base) / HD))
    sine = jnp.sin(angles)
    tables[:requests] = jnp.cos(angles)
    tables[requests:] = jnp.where(lane < HALF, -sine, sine)
    mine = lax.div(device[0], 2)
    keys_here = lax.rem(device[0], 2) == 0
    own_tables[0:1, :] = jnp.where(keys_here, tables[pl.ds(mine, 1), :], 1.0)
    own_tables[1:2, :] = jnp.where(keys_here, tables[pl.ds(requests + mine, 1), :], 0.0)
    place_slots(device[0], lengths, table, pair_of, live, slots, 2 * chips * slots)


def normalize_kernel(device, near, far, square, gain, w_kv, normed, kept, away):
    chips, requests, width = near.shape
    n = 2 * chips
    core = lax.rem(device[0], 2)
    total = square[...]
    for chip in range(chips):
        values = far[chip].astype(f32)
        total = total + values * values
    scale = lax.rsqrt(jnp.sum(total, axis=1, keepdims=True) / (n * width) + 1e-05)
    for k in range(n):
        chip, from_core = divmod(k, 2)
        values = jnp.where(core == from_core, near[chip].astype(f32), far[chip].astype(f32))
        normed[k] = (values * scale * gain[:, k * width : (k + 1) * width]).astype(bf16)
    own = normed[device[0]]
    for result, half in ((kept, core), (away, 1 - core)):
        columns = pl.ds(pl.multiple_of(half * KV, KV), KV)
        result[...] = jnp.dot(own, w_kv[:, columns], preferred_element_type=f32)


def query_kernel(normed, tables, w_query, query):
    n, requests, width = normed.shape
    columns = w_query.shape[1]
    product = jnp.zeros((requests, columns), f32)
    for k in range(n):
        product = product + jnp.dot(
            normed[k], w_query[k * width : (k + 1) * width, :], preferred_element_type=f32
        )
    cosine, sine = tables[:requests], tables[requests:]
    for c in range(columns // HD):
        turned = rotate(product[:, c * HD : (c + 1) * HD], cosine, sine)
        query[:, c * HD : (c + 1) * HD] = turned.astype(bf16)


def gather_kernel(query, kept, came, send, kv_rows):
    chips, requests, wide = send.shape
    columns = wide - HD
    for group in range(KVH):
        part = slice(group * HD, (group + 1) * HD)
        value = kept[:, part] + came[:, part]
        upper = value.astype(bf16).astype(f32)
        kv_rows[pl.ds(group, requests, stride=2 * KVH), :] = upper
        kv_rows[pl.ds(KVH + group, requests, stride=2 * KVH), :] = value - upper
    whole = query[...]
    for chip in range(chips):
        send[chip, :, :columns] = whole
        rows = kv_rows[chip * 2 * KVH : (chip + 1) * 2 * KVH, :]
        if requests > 2 * KVH:
            rows = jnp.concatenate([rows, jnp.zeros((requests - 2 * KVH, HD), f32)], axis=0)
        send[chip, :, columns:] = rows.astype(bf16)


def entry_kernel(got, own_tables, row):
    columns = got.shape[2] - HD
    kv = jnp.zeros((2 * KVH, HD), f32)
    for chip in range(got.shape[0]):
        kv = kv + got[chip, : 2 * KVH, columns:].astype(f32)
    kv = kv + pltpu.roll(kv, KVH, 0)
    row[...] = rotate(kv, own_tables[0:1, :], own_tables[1:2, :]).astype(bf16)


def attend_kernel(
    pair_of, live, got, k_near, v_near, k_far, v_far, peak, total, mixed,
    queries, slot_score, slot_out, slot_peak, slot_total, run_peak, run_total, run_mixed,
):
    chips, requests, wide = got.shape
    heads = (wide - HD) // HD
    slots, page = k_near.shape[:2]
    pairs = requests * KVH
    for h in range(CORE_H):
        chip, c = divmod(h, heads)
        queries[pl.ds(h, requests, stride=CORE_H), :] = got[
            chip, :, c * HD : (c + 1) * HD
        ].astype(f32)
    queries[pairs * CORE_GH :, :] = jnp.zeros((CORE_GH, HD), f32)
    run_peak[...] = jnp.full_like(run_peak, lowest)
    run_total[...] = jnp.zeros_like(run_total)
    run_mixed[...] = jnp.zeros_like(run_mixed)

    def rows_of(s, side=0):
        start = (pair_of[0, s] + side * (pairs + 1)) * CORE_GH
        return pl.ds(pl.multiple_of(start, CORE_GH), CORE_GH)

    for s in range(2 * slots):
        keys = k_near[s] if s < slots else k_far[s - slots]
        slot_score[s] = lax.dot_general(
            queries[rows_of(s), :].astype(bf16), keys, (((1,), (1,)), ((), ())),
            preferred_element_type=f32,
        )
    shape = (CORE_GH, HD)
    places = lane_of((CORE_GH, page))
    for s in range(2 * slots):
        alive = places < live[0, s]
        scores = jnp.where(alive, slot_score[s] * score_scale, lowest)
        top = jnp.max(scores, axis=1, keepdims=True)
        weights = jnp.where(alive, jnp.exp(scores - top), 0.0)
        slot_score[s] = weights
        slot_peak[s] = jnp.broadcast_to(top, shape)
        slot_total[s] = jnp.broadcast_to(jnp.sum(weights, axis=1, keepdims=True), shape)
    for s in range(2 * slots):
        values = v_near[s] if s < slots else v_far[s - slots]
        slot_out[s] = jnp.dot(slot_score[s].astype(bf16), values, preferred_element_type=f32)
    for side in range(2):
        running = jnp.full(shape, lowest, f32)
        for s in range(side * slots, (side + 1) * slots):
            if s > side * slots:
                same = pair_of[0, s] == pair_of[0, s - 1]
                running = jnp.where(same, running, lowest)
            running = jnp.maximum(slot_peak[s], running)
            run_peak[rows_of(s, side), :] = running
    for side in range(2):
        sum_total = jnp.zeros(shape, f32)
        sum_mixed = jnp.zeros(shape, f32)
        for s in range(side * slots, (side + 1) * slots):
            if s > side * slots:
                keep = jnp.where(pair_of[0, s] == pair_of[0, s - 1], 1.0, 0.0)
                sum_total, sum_mixed = keep * sum_total, keep * sum_mixed
            rows = rows_of(s, side)
            factor = jnp.exp(slot_peak[s] - run_peak[rows, :])
            sum_total = sum_total + factor * slot_total[s]
            sum_mixed = sum_mixed + factor * slot_out[s]
            run_total[rows, :] = sum_total
            run_mixed[rows, :] = sum_mixed
    for pair in range(pairs):
        here = slice(pair * CORE_GH, (pair + 1) * CORE_GH)
        first = run_peak[here, :]
        there = slice((pairs + 1 + pair) * CORE_GH, (pairs + 2 + pair) * CORE_GH)
        second = run_peak[there, :]
        top = jnp.maximum(first, second)
        first, second = jnp.exp(first - top), jnp.exp(second - top)
        peak[here, :] = top
        total[here, :] = first * run_total[here, :] + second * run_total[there, :]
        mixed[here, :] = first * run_mixed[here, :] + second * run_mixed[there, :]


def share_kernel(device, peak, total, mixed, near_row, far_row, send, kv_block):
    chips, requests, wide = send.shape
    columns = wide - 2 * HD
    heads = columns // HD
    core = lax.rem(device[0], 2)
    near, far = near_row[...].astype(f32), far_row[...].astype(f32)
    keys_here = lax.broadcasted_iota(jnp.int32, near.shape, 0) < KVH
    own = jnp.where(core == 0, near, far)
    other = jnp.where(core == 0, far, near)
    if requests > 2 * KVH:
        kv_block[...] = jnp.zeros_like(kv_block)
    kv_block[: 2 * KVH, :] = jnp.where(keys_here, own, other)
    lanes = lane_of((requests, HD))
    order = lax.rem(lanes, heads)
    kind = lax.div(lanes, heads)
    kinds = lax.rem(kind, 3)
    for chip in range(chips):
        stats = jnp.zeros((requests, HD), f32)
        for c in range(heads):
            rows = pl.ds(chip * heads + c, requests, stride=CORE_H)
            send[chip, :, c * HD : (c + 1) * HD] = mixed[rows, :].astype(bf16)
            value = jnp.where(kind < 3, peak[rows, :], total[rows, :])
            stats = jnp.where(order == c, value, stats)
        first = stats.astype(bf16).astype(f32)
        stats = stats - first
        second = stats.astype(bf16).astype(f32)
        third = stats - second
        stats = jnp.where(kinds == 0, first, jnp.where(kinds == 1, second, third))
        send[chip, :, columns : columns + HD] = stats.astype(bf16)
        send[chip, :, columns + HD :] = kv_block[...].astype(bf16)


def multiply_out(attention, w_out, result, core):
    chips, _, width = result.shape
    whole = attention[...]
    for chip in range(chips):
        columns = pl.ds(pl.multiple_of((2 * chip + core) * width, HD), width)
        result[chip] = jnp.dot(
            whole, w_out[:, columns], preferred_element_type=f32
        ).astype(result.dtype)


def combine_kernel(device, got, query, w_out, away, new_entries, attention, entries):
    chips, requests, wide = got.shape
    columns = wide - 2 * HD
    heads = columns // HD
    lanes = lane_of((requests, HD))
    for request in range(requests):
        block = got[request, : 2 * KVH, columns + HD :].astype(f32)
        entries[pl.ds(request, 2 * KVH, stride=requests), :] = block
    for i in range(2 * KVH):
        new_entries[:, i * HD : (i + 1) * HD] = entries[
            i * requests : (i + 1) * requests, :
        ].astype(bf16)

    def own(c, half):
        start = (lax.div(device[0] * heads + c, GH) + half * KVH) * requests
        return entries[pl.ds(pl.multiple_of(start, 8), requests), :]

    new_score = jnp.full((requests, HD), lowest, f32)
    for c in range(heads):
        score = query[:, c * HD : (c + 1) * HD].astype(f32) * own(c, 0)
        score = jnp.sum(score, axis=1, keepdims=True) * score_scale
        new_score = jnp.where(lanes == c, score, new_score)
    peaks, totals = [], []
    for src in range(chips):
        stats = got[src, :, columns : columns + HD].astype(f32)
        stats = (
            stats + pltpu.roll(stats, HD - heads, 1) + pltpu.roll(stats, HD - 2 * heads, 1)
        )
        peaks.append(stats)
        totals.append(pltpu.roll(stats, HD - 3 * heads, 1))
    top = new_score
    for value in peaks:
        top = jnp.maximum(top, value)
    weights = [jnp.exp(value - top) for value in peaks]
    new_weight = jnp.exp(new_score - top)
    total = new_weight
    for weight, value in zip(weights, totals):
        total = total + weight * value
    inverse = 1.0 / total
    weights = [weight * inverse for weight in weights]
    new_weight = new_weight * inverse
    for c in range(heads):
        mixed = new_weight[:, c : c + 1] * own(c, 1)
        for src in range(chips):
            mixed = mixed + weights[src][:, c : c + 1] * got[
                src, :, c * HD : (c + 1) * HD
            ].astype(f32)
        attention[:, c * HD : (c + 1) * HD] = mixed.astype(bf16)
    multiply_out(attention, w_out, away, 1 - lax.rem(device[0], 2))


def keep_kernel(device, attention, w_out, kept):
    multiply_out(attention, w_out, kept, lax.rem(device[0], 2))


def join_kernel(kept, came, send):
    for chip in range(send.shape[0]):
        send[chip] = (kept[chip] + came[chip].astype(f32)).astype(bf16)


def call(kernel, out_shape, in_spaces, out_spaces, scratch, limit, moved=None):
    return pl.pallas_call(
        kernel,
        out_shape=out_shape,
        in_specs=[pl.BlockSpec(memory_space=space) for space in in_spaces],
        out_specs=[pl.BlockSpec(memory_space=space) for space in out_spaces],
        scratch_shapes=scratch,
        compiler_params=pltpu.CompilerParams(vmem_limit_bytes=limit << 20),
        cost_estimate=moved
        and pl.CostEstimate(flops=moved * 512, bytes_accessed=moved, transcendentals=0),
    )


def local(hidden, gain, w_query, w_kv, w_out, k_cache, v_cache, block_table, lengths):
    device = lax.axis_index("attn").astype(jnp.int32).reshape(1)
    n = lax.axis_size("attn")
    requests, width = hidden.shape
    columns = w_query.shape[1]
    slots = k_cache.shape[0]
    pairs = requests * KVH
    assert 2 * requests == n

    shape = jax.ShapeDtypeStruct
    halves = shape((n // 2, requests, width), bf16)
    (send,) = call(
        spread_kernel,
        [halves],
        [SMEM, VMEM],
        [VMEM],
        [],
        2,
        2 * (w_query.nbytes + w_kv.nbytes),
    )(device, hidden)
    near = exchange(send)
    far = swap_cores(near)
    tables, own_tables, pair_of, live, square = call(
        functools.partial(prepare_kernel, slots=slots),
        [
            shape((2 * requests, HD), f32),
            shape((2, HD), f32),
            shape((1, HD), jnp.int32),
            shape((1, HD), jnp.int32),
            shape((requests, width), f32),
        ],
        [SMEM] * 3 + [VMEM],
        [VMEM] * 5,
        [],
        2,
    )(device, lengths, block_table, near)
    half_kv = shape((requests, KV), f32)
    normed, kept, away = call(
        normalize_kernel,
        [shape((n, requests, width), bf16), half_kv, half_kv],
        [SMEM] + [VMEM] * 5,
        [VMEM] * 3,
        [],
        4,
    )(device, near, far, square, gain.reshape(1, n * width), w_kv)
    came = swap_cores(away)
    (query,) = call(
        query_kernel, [shape((requests, columns), bf16)], [VMEM] * 3, [VMEM], [], 4
    )(normed, tables, w_query)
    (send,) = call(
        gather_kernel,
        [shape((n // 2, requests, columns + HD), bf16)],
        [VMEM] * 3,
        [VMEM],
        [pltpu.VMEM((requests * 2 * KVH, HD), f32)],
        4,
    )(query, kept, came)
    k_far, v_far = swap_cores(k_cache), swap_cores(v_cache)
    got = exchange(send)
    (near_row,) = call(entry_kernel, [shape((2 * KVH, HD), bf16)], [VMEM] * 2, [VMEM], [], 2)(
        got, own_tables
    )
    far_row = swap_cores(near_row)
    rows = shape((pairs * CORE_GH, HD), f32)
    slot_rows = pltpu.VMEM((2 * slots, CORE_GH, HD), f32)
    run_rows = pltpu.VMEM((2 * (pairs + 1) * CORE_GH, HD), f32)
    peak, total, mixed = call(
        attend_kernel,
        [rows] * 3,
        [SMEM] * 2 + [VMEM] * 5,
        [VMEM] * 3,
        [pltpu.VMEM(((pairs + 1) * CORE_GH, HD), f32)] + [slot_rows] * 4 + [run_rows] * 3,
        8,
    )(pair_of, live, got, k_cache, v_cache, k_far, v_far)
    (send,) = call(
        share_kernel,
        [shape((n // 2, requests, columns + 2 * HD), bf16)],
        [SMEM] + [VMEM] * 5,
        [VMEM],
        [pltpu.VMEM((requests, HD), f32)],
        4,
    )(device, peak, total, mixed, near_row, far_row)
    got = exchange(send)
    away, new_entries, attention = call(
        combine_kernel,
        [halves, shape((requests, 2 * KV), bf16), shape((requests, columns), bf16)],
        [SMEM] + [VMEM] * 3,
        [VMEM] * 3,
        [pltpu.VMEM((2 * KVH * requests, HD), f32)],
        4,
    )(device, got, query, w_out)
    came = swap_cores(away)
    (kept,) = call(
        keep_kernel, [shape(halves.shape, f32)], [SMEM] + [VMEM] * 2, [VMEM], [], 4
    )(device, attention, w_out)
    (send,) = call(join_kernel, [halves], [VMEM] * 2, [VMEM], [], 4)(kept, came)
    got = exchange(send)
    (attn_out,) = call(add_kernel, [shape((requests, width), bf16)], [VMEM], [VMEM], [], 4)(got)
    return attn_out, new_entries


def solution(mesh):
    in_specs = (
        P("groups", "attn"),
        P(),
        P(None, "attn"),
        P("attn", None),
        P("attn", None),
        P(("groups", "attn"), None, None),
        P(("groups", "attn"), None, None),
        P("groups", None, None),
        P("groups"),
    )
    out_specs = (P("groups", "attn"), P("groups", None))
    return jax.shard_map(local, mesh=mesh, in_specs=in_specs, out_specs=out_specs, check_vma=False)
```

```python
import functools
import math

import jax
import jax.numpy as jnp
from jax import lax
from jax.experimental import pallas as pl
from jax.experimental.pallas import tpu as pltpu
from jax.sharding import PartitionSpec as P

HD = 128
H = 64
KVH = 4
GH = H // KVH
CORE_H = H // 2
CORE_GH = GH // 2

lowest = -1e30
rope_base = 500000.0
score_scale = 1.0 / math.sqrt(HD)
bf16 = jnp.bfloat16
f32 = jnp.float32
VMEM = pltpu.MemorySpace.VMEM
SMEM = pltpu.MemorySpace.SMEM
KV = KVH * HD
PAGE = 128
HALF = HD // 2


def rotate(vectors, cosine, sine):
    return vectors * cosine + pltpu.roll(vectors, HALF, 1) * sine


def exchange(buffer):
    chips = buffer.shape[0]
    groups = [[2 * chip + core for chip in range(chips)] for core in range(2)]
    return lax.all_to_all(buffer, "attn", 0, 0, tiled=True, axis_index_groups=groups)


def swap_cores(buffer):
    n = lax.axis_size("attn")
    return lax.ppermute(buffer, "attn", [(i, i ^ 1) for i in range(n)])


def lane_of(shape):
    return lax.broadcasted_iota(jnp.int32, shape, 1)


def spread_kernel(device, hidden, send):
    for j in range(send.shape[0]):
        send[j] = hidden[...]


def add_kernel(got, entries, out, new_entries):
    total = got[0].astype(f32)
    for src in range(1, got.shape[0]):
        total = total + got[src].astype(f32)
    out[...] = total.astype(bf16)
    requests = out.shape[0]
    for i in range(2 * KVH):
        rows = slice(i * requests, (i + 1) * requests)
        new_entries[:, i * HD : (i + 1) * HD] = entries[rows, :].astype(bf16)


def place_slots(device, lengths, table, pair_of, live, slots, total):
    requests = table.shape[0]
    lane = lane_of((1, HD))
    partner = device + 1 - 2 * lax.rem(device, 2)
    slot = jnp.where(lane < slots, device * slots + lane, (partner - 1) * slots + lane)
    pair = jnp.full((1, HD), requests * KVH, jnp.int32)
    alive = jnp.zeros((1, HD), jnp.int32)
    for r in range(requests):
        pages = lax.div(lengths[r] + PAGE - 1, PAGE)
        offset = slot - table[r, 0, 0]
        offset = jnp.where(offset < 0, offset + total, offset)
        here = offset < KVH * pages
        group = jnp.zeros((1, HD), jnp.int32)
        for g in range(1, KVH):
            group = group + (offset >= g * pages).astype(jnp.int32)
        pair = jnp.where(here, r * KVH + group, pair)
        alive = jnp.where(here, lengths[r] - 1 - (offset - group * pages) * PAGE, alive)
    pair_of[...] = pair
    live[...] = alive


def prepare_kernel(
    device, lengths, table, near, tables, own_tables, pair_of, live, square, *, slots
):
    chips, requests, _ = near.shape
    total = jnp.zeros(square.shape, f32)
    for chip in range(chips):
        values = near[chip].astype(f32)
        total = total + values * values
    square[...] = total
    row, lane = lax.broadcasted_iota(jnp.int32, (requests, HD), 0), lane_of((requests, HD))
    position = jnp.zeros((requests, HD), f32)
    for r in range(requests):
        position = jnp.where(row == r, (lengths[r] - 1).astype(f32), position)
    index = jnp.where(lane < HALF, lane, lane - HALF).astype(f32)
    angles = position * jnp.exp(index * (-2.0 * math.log(rope_base) / HD))
    sine = jnp.sin(angles)
    tables[:requests] = jnp.cos(angles)
    tables[requests:] = jnp.where(lane < HALF, -sine, sine)
    mine = lax.div(device[0], 2)
    keys_here = lax.rem(device[0], 2) == 0
    own_tables[0:1, :] = jnp.where(keys_here, tables[pl.ds(mine, 1), :], 1.0)
    own_tables[1:2, :] = jnp.where(keys_here, tables[pl.ds(requests + mine, 1), :], 0.0)
    place_slots(device[0], lengths, table, pair_of, live, slots, 2 * chips * slots)


def normalize_kernel(device, near, far, square, gain, w_kv, normed, kept, away):
    chips, requests, width = near.shape
    n = 2 * chips
    core = lax.rem(device[0], 2)
    total = square[...]
    for chip in range(chips):
        values = far[chip].astype(f32)
        total = total + values * values
    scale = lax.rsqrt(jnp.sum(total, axis=1, keepdims=True) / (n * width) + 1e-05)
    for k in range(n):
        chip, from_core = divmod(k, 2)
        values = jnp.where(core == from_core, near[chip].astype(f32), far[chip].astype(f32))
        normed[k] = (values * scale * gain[:, k * width : (k + 1) * width]).astype(bf16)
    own = normed[device[0]]
    for result, half in ((kept, core), (away, 1 - core)):
        columns = pl.ds(pl.multiple_of(half * KV, KV), KV)
        result[...] = jnp.dot(own, w_kv[:, columns], preferred_element_type=f32)


def query_kernel(normed, tables, w_query, query):
    n, requests, width = normed.shape
    columns = w_query.shape[1]
    product = jnp.zeros((requests, columns), f32)
    for k in range(n):
        product = product + jnp.dot(
            normed[k], w_query[k * width : (k + 1) * width, :], preferred_element_type=f32
        )
    cosine, sine = tables[:requests], tables[requests:]
    for c in range(columns // HD):
        turned = rotate(product[:, c * HD : (c + 1) * HD], cosine, sine)
        query[:, c * HD : (c + 1) * HD] = turned.astype(bf16)


def gather_kernel(query, kept, came, send, kv_rows):
    chips, requests, wide = send.shape
    columns = wide - HD
    for group in range(KVH):
        part = slice(group * HD, (group + 1) * HD)
        value = kept[:, part] + came[:, part]
        upper = value.astype(bf16).astype(f32)
        kv_rows[pl.ds(group, requests, stride=2 * KVH), :] = upper
        kv_rows[pl.ds(KVH + group, requests, stride=2 * KVH), :] = value - upper
    whole = query[...]
    for chip in range(chips):
        send[chip, :, :columns] = whole
        rows = kv_rows[chip * 2 * KVH : (chip + 1) * 2 * KVH, :]
        if requests > 2 * KVH:
            rows = jnp.concatenate([rows, jnp.zeros((requests - 2 * KVH, HD), f32)], axis=0)
        send[chip, :, columns:] = rows.astype(bf16)


def entry_kernel(got, own_tables, row):
    columns = got.shape[2] - HD
    kv = jnp.zeros((2 * KVH, HD), f32)
    for chip in range(got.shape[0]):
        kv = kv + got[chip, : 2 * KVH, columns:].astype(f32)
    kv = kv + pltpu.roll(kv, KVH, 0)
    row[...] = rotate(kv, own_tables[0:1, :], own_tables[1:2, :]).astype(bf16)


def attend_kernel(
    pair_of, live, got, k_near, v_near, k_far, v_far, peak, total, mixed,
    queries, slot_score, slot_out, slot_peak, slot_total, run_peak, run_total, run_mixed,
):
    chips, requests, wide = got.shape
    heads = (wide - HD) // HD
    slots, page = k_near.shape[:2]
    pairs = requests * KVH
    for h in range(CORE_H):
        chip, c = divmod(h, heads)
        queries[pl.ds(h, requests, stride=CORE_H), :] = got[
            chip, :, c * HD : (c + 1) * HD
        ].astype(f32)
    queries[pairs * CORE_GH :, :] = jnp.zeros((CORE_GH, HD), f32)
    run_peak[...] = jnp.full_like(run_peak, lowest)
    run_total[...] = jnp.zeros_like(run_total)
    run_mixed[...] = jnp.zeros_like(run_mixed)

    def rows_of(s, side=0):
        start = (pair_of[0, s] + side * (pairs + 1)) * CORE_GH
        return pl.ds(pl.multiple_of(start, CORE_GH), CORE_GH)

    for s in range(0, 2 * slots, 2):
        pages, at = (k_near, s) if s < slots else (k_far, s - slots)
        both = jnp.concatenate([queries[rows_of(s), :], queries[rows_of(s + 1), :]], axis=0)
        scores = lax.dot_general(
            both.astype(bf16), pages[at : at + 2].reshape(2 * page, HD), (((1,), (1,)), ((), ())),
            preferred_element_type=f32,
        )
        slot_score[s] = scores[:CORE_GH, :page]
        slot_score[s + 1] = scores[CORE_GH:, page:]
    shape = (CORE_GH, HD)
    places = lane_of((CORE_GH, page))
    for s in range(2 * slots):
        alive = places < live[0, s]
        scores = jnp.where(alive, slot_score[s] * score_scale, lowest)
        top = jnp.max(scores, axis=1, keepdims=True)
        weights = jnp.where(alive, jnp.exp(scores - top), 0.0)
        slot_score[s] = weights
        slot_peak[s] = jnp.broadcast_to(top, shape)
        slot_total[s] = jnp.broadcast_to(jnp.sum(weights, axis=1, keepdims=True), shape)
    for s in range(2 * slots):
        values = v_near[s] if s < slots else v_far[s - slots]
        slot_out[s] = jnp.dot(slot_score[s].astype(bf16), values, preferred_element_type=f32)
    running = [jnp.full(shape, lowest, f32)] * 2
    for t in range(slots):
        for side in range(2):
            s = side * slots + t
            if t:
                same = pair_of[0, s] == pair_of[0, s - 1]
                running[side] = jnp.where(same, running[side], lowest)
            running[side] = jnp.maximum(slot_peak[s], running[side])
            run_peak[rows_of(s, side), :] = running[side]
    for s in range(2 * slots):
        slot_peak[s] = jnp.exp(slot_peak[s] - run_peak[rows_of(s, s // slots), :])
    sum_total = [jnp.zeros(shape, f32)] * 2
    sum_mixed = [jnp.zeros(shape, f32)] * 2
    for t in range(slots):
        for side in range(2):
            s = side * slots + t
            if t:
                keep = jnp.where(pair_of[0, s] == pair_of[0, s - 1], 1.0, 0.0)
                sum_total[side], sum_mixed[side] = keep * sum_total[side], keep * sum_mixed[side]
            rows, factor = rows_of(s, side), slot_peak[s]
            sum_total[side] = sum_total[side] + factor * slot_total[s]
            sum_mixed[side] = sum_mixed[side] + factor * slot_out[s]
            run_total[rows, :] = sum_total[side]
            run_mixed[rows, :] = sum_mixed[side]
    for pair in range(pairs):
        here = slice(pair * CORE_GH, (pair + 1) * CORE_GH)
        first = run_peak[here, :]
        there = slice((pairs + 1 + pair) * CORE_GH, (pairs + 2 + pair) * CORE_GH)
        second = run_peak[there, :]
        top = jnp.maximum(first, second)
        first, second = jnp.exp(first - top), jnp.exp(second - top)
        peak[here, :] = top
        total[here, :] = first * run_total[here, :] + second * run_total[there, :]
        mixed[here, :] = first * run_mixed[here, :] + second * run_mixed[there, :]


def share_kernel(device, peak, total, mixed, near_row, far_row, send, kv_block):
    chips, requests, wide = send.shape
    columns = wide - 2 * HD
    heads = columns // HD
    core = lax.rem(device[0], 2)
    near, far = near_row[...].astype(f32), far_row[...].astype(f32)
    keys_here = lax.broadcasted_iota(jnp.int32, near.shape, 0) < KVH
    own = jnp.where(core == 0, near, far)
    other = jnp.where(core == 0, far, near)
    if requests > 2 * KVH:
        kv_block[...] = jnp.zeros_like(kv_block)
    kv_block[: 2 * KVH, :] = jnp.where(keys_here, own, other)
    lanes = lane_of((requests, HD))
    order = lax.rem(lanes, heads)
    kind = lax.div(lanes, heads)
    kinds = lax.rem(kind, 3)
    for chip in range(chips):
        stats = jnp.zeros((requests, HD), f32)
        for c in range(heads):
            rows = pl.ds(chip * heads + c, requests, stride=CORE_H)
            send[chip, :, c * HD : (c + 1) * HD] = mixed[rows, :].astype(bf16)
            value = jnp.where(kind < 3, peak[rows, :], total[rows, :])
            stats = jnp.where(order == c, value, stats)
        first = stats.astype(bf16).astype(f32)
        stats = stats - first
        second = stats.astype(bf16).astype(f32)
        third = stats - second
        stats = jnp.where(kinds == 0, first, jnp.where(kinds == 1, second, third))
        send[chip, :, columns : columns + HD] = stats.astype(bf16)
        send[chip, :, columns + HD :] = kv_block[...].astype(bf16)


def multiply_out(attention, w_out, result, core):
    chips, _, width = result.shape
    whole = attention[...]
    for chip in range(chips):
        columns = pl.ds(pl.multiple_of((2 * chip + core) * width, HD), width)
        result[chip] = jnp.dot(
            whole, w_out[:, columns], preferred_element_type=f32
        ).astype(result.dtype)


def combine_kernel(device, got, query, w_out, away, attention, entries):
    chips, requests, wide = got.shape
    columns = wide - 2 * HD
    heads = columns // HD
    lanes = lane_of((requests, HD))
    for request in range(requests):
        block = got[request, : 2 * KVH, columns + HD :].astype(f32)
        entries[pl.ds(request, 2 * KVH, stride=requests), :] = block

    def own(c, half):
        start = (lax.div(device[0] * heads + c, GH) + half * KVH) * requests
        return entries[pl.ds(pl.multiple_of(start, 8), requests), :]

    new_score = jnp.full((requests, HD), lowest, f32)
    for c in range(heads):
        score = query[:, c * HD : (c + 1) * HD].astype(f32) * own(c, 0)
        score = jnp.sum(score, axis=1, keepdims=True) * score_scale
        new_score = jnp.where(lanes == c, score, new_score)
    peaks, totals = [], []
    for src in range(chips):
        stats = got[src, :, columns : columns + HD].astype(f32)
        stats = (
            stats + pltpu.roll(stats, HD - heads, 1) + pltpu.roll(stats, HD - 2 * heads, 1)
        )
        peaks.append(stats)
        totals.append(pltpu.roll(stats, HD - 3 * heads, 1))
    top = new_score
    for value in peaks:
        top = jnp.maximum(top, value)
    weights = [jnp.exp(value - top) for value in peaks]
    new_weight = jnp.exp(new_score - top)
    total = new_weight
    for weight, value in zip(weights, totals):
        total = total + weight * value
    inverse = 1.0 / total
    weights = [weight * inverse for weight in weights]
    new_weight = new_weight * inverse
    for c in range(heads):
        mixed = new_weight[:, c : c + 1] * own(c, 1)
        for src in range(chips):
            mixed = mixed + weights[src][:, c : c + 1] * got[
                src, :, c * HD : (c + 1) * HD
            ].astype(f32)
        attention[:, c * HD : (c + 1) * HD] = mixed.astype(bf16)
    multiply_out(attention, w_out, away, 1 - lax.rem(device[0], 2))


def keep_kernel(device, attention, w_out, kept):
    multiply_out(attention, w_out, kept, lax.rem(device[0], 2))


def join_kernel(kept, came, send):
    for chip in range(send.shape[0]):
        send[chip] = (kept[chip] + came[chip].astype(f32)).astype(bf16)


def call(kernel, out_shape, in_spaces, out_spaces, scratch, limit, moved=None):
    return pl.pallas_call(
        kernel,
        out_shape=out_shape,
        in_specs=[pl.BlockSpec(memory_space=space) for space in in_spaces],
        out_specs=[pl.BlockSpec(memory_space=space) for space in out_spaces],
        scratch_shapes=scratch,
        compiler_params=pltpu.CompilerParams(vmem_limit_bytes=limit << 20),
        cost_estimate=moved
        and pl.CostEstimate(flops=moved * 512, bytes_accessed=moved, transcendentals=0),
    )


def local(hidden, gain, w_query, w_kv, w_out, k_cache, v_cache, block_table, lengths):
    device = lax.axis_index("attn").astype(jnp.int32).reshape(1)
    n = lax.axis_size("attn")
    requests, width = hidden.shape
    columns = w_query.shape[1]
    slots = k_cache.shape[0]
    pairs = requests * KVH
    assert 2 * requests == n and slots % 2 == 0 and 2 * slots <= HD

    shape = jax.ShapeDtypeStruct
    halves = shape((n // 2, requests, width), bf16)
    device, k_cache, v_cache = lax.optimization_barrier((device, k_cache, v_cache))
    k_far, v_far = swap_cores(k_cache), swap_cores(v_cache)
    (send,) = call(
        spread_kernel,
        [halves],
        [SMEM, VMEM],
        [VMEM],
        [],
        2,
        2 * (w_query.nbytes + w_kv.nbytes),
    )(device, hidden)
    near = exchange(send)
    far = swap_cores(near)
    tables, own_tables, pair_of, live, square = call(
        functools.partial(prepare_kernel, slots=slots),
        [
            shape((2 * requests, HD), f32),
            shape((2, HD), f32),
            shape((1, HD), jnp.int32),
            shape((1, HD), jnp.int32),
            shape((requests, width), f32),
        ],
        [SMEM] * 3 + [VMEM],
        [VMEM] * 5,
        [],
        2,
    )(device, lengths, block_table, near)
    half_kv = shape((requests, KV), f32)
    normed, kept, away = call(
        normalize_kernel,
        [shape((n, requests, width), bf16), half_kv, half_kv],
        [SMEM] + [VMEM] * 5,
        [VMEM] * 3,
        [],
        4,
    )(device, near, far, square, gain.reshape(1, n * width), w_kv)
    came = swap_cores(away)
    (query,) = call(
        query_kernel, [shape((requests, columns), bf16)], [VMEM] * 3, [VMEM], [], 4
    )(normed, tables, w_query)
    (send,) = call(
        gather_kernel,
        [shape((n // 2, requests, columns + HD), bf16)],
        [VMEM] * 3,
        [VMEM],
        [pltpu.VMEM((requests * 2 * KVH, HD), f32)],
        4,
    )(query, kept, came)
    got = exchange(send)
    (near_row,) = call(entry_kernel, [shape((2 * KVH, HD), bf16)], [VMEM] * 2, [VMEM], [], 2)(
        got, own_tables
    )
    far_row = swap_cores(near_row)
    rows = shape((pairs * CORE_GH, HD), f32)
    slot_rows = pltpu.VMEM((2 * slots, CORE_GH, HD), f32)
    run_rows = pltpu.VMEM((2 * (pairs + 1) * CORE_GH, HD), f32)
    peak, total, mixed = call(
        attend_kernel,
        [rows] * 3,
        [SMEM] * 2 + [VMEM] * 5,
        [VMEM] * 3,
        [pltpu.VMEM(((pairs + 1) * CORE_GH, HD), f32)] + [slot_rows] * 4 + [run_rows] * 3,
        8,
    )(pair_of, live, got, k_cache, v_cache, k_far, v_far)
    (send,) = call(
        share_kernel,
        [shape((n // 2, requests, columns + 2 * HD), bf16)],
        [SMEM] + [VMEM] * 5,
        [VMEM],
        [pltpu.VMEM((requests, HD), f32)],
        4,
    )(device, peak, total, mixed, near_row, far_row)
    got = exchange(send)
    away, attention, entries = call(
        combine_kernel,
        [
            halves,
            shape((requests, columns), bf16),
            shape((2 * KVH * requests, HD), f32),
        ],
        [SMEM] + [VMEM] * 3,
        [VMEM] * 3,
        [],
        4,
    )(device, got, query, w_out)
    came = swap_cores(away)
    (kept,) = call(
        keep_kernel, [shape(halves.shape, f32)], [SMEM] + [VMEM] * 2, [VMEM], [], 4
    )(device, attention, w_out)
    (send,) = call(join_kernel, [halves], [VMEM] * 2, [VMEM], [], 4)(kept, came)
    got = exchange(send)
    attn_out, new_entries = call(
        add_kernel,
        [shape((requests, width), bf16), shape((requests, 2 * KV), bf16)],
        [VMEM] * 2,
        [VMEM] * 2,
        [],
        4,
    )(got, entries)
    return attn_out, new_entries


def solution(mesh):
    in_specs = (
        P("groups", "attn"),
        P(),
        P(None, "attn"),
        P("attn", None),
        P("attn", None),
        P(("groups", "attn"), None, None),
        P(("groups", "attn"), None, None),
        P("groups", None, None),
        P("groups"),
    )
    out_specs = (P("groups", "attn"), P("groups", None))
    return jax.shard_map(local, mesh=mesh, in_specs=in_specs, out_specs=out_specs, check_vma=False)
```

```python
import functools
import math

import jax
import jax.numpy as jnp
from jax import lax
from jax.experimental import pallas as pl
from jax.experimental.pallas import tpu as pltpu
from jax.sharding import PartitionSpec as P

HD = 128
H = 64
KVH = 4
GH = H // KVH
CORE_H = H // 2
CORE_GH = GH // 2

lowest = -1e30
rope_base = 500000.0
score_scale = 1.0 / math.sqrt(HD)
bf16 = jnp.bfloat16
f32 = jnp.float32
VMEM = pltpu.MemorySpace.VMEM
SMEM = pltpu.MemorySpace.SMEM
KV = KVH * HD
PAGE = 128
HALF = HD // 2


def rotate(vectors, cosine, sine):
    return vectors * cosine + pltpu.roll(vectors, HALF, 1) * sine


def exchange(buffer):
    chips = buffer.shape[0]
    groups = [[2 * chip + core for chip in range(chips)] for core in range(2)]
    return lax.all_to_all(buffer, "attn", 0, 0, tiled=True, axis_index_groups=groups)


def swap_cores(buffer):
    n = lax.axis_size("attn")
    return lax.ppermute(buffer, "attn", [(i, i ^ 1) for i in range(n)])


def lane_of(shape):
    return lax.broadcasted_iota(jnp.int32, shape, 1)


def spread_kernel(device, hidden, send):
    for j in range(send.shape[0]):
        send[j] = hidden[...]


def add_kernel(got, entries, out, new_entries):
    total = got[0].astype(f32)
    for src in range(1, got.shape[0]):
        total = total + got[src].astype(f32)
    out[...] = total.astype(bf16)
    requests = out.shape[0]
    for i in range(2 * KVH):
        rows = slice(i * requests, (i + 1) * requests)
        new_entries[:, i * HD : (i + 1) * HD] = entries[rows, :].astype(bf16)


def place_slots(device, lengths, table, pair_of, live, slots, total):
    requests = table.shape[0]
    lane = lane_of((1, HD))
    partner = device + 1 - 2 * lax.rem(device, 2)
    slot = jnp.where(lane < slots, device * slots + lane, (partner - 1) * slots + lane)
    pair = jnp.full((1, HD), requests * KVH, jnp.int32)
    alive = jnp.zeros((1, HD), jnp.int32)
    for r in range(requests):
        pages = lax.div(lengths[r] + PAGE - 1, PAGE)
        offset = slot - table[r, 0, 0]
        offset = jnp.where(offset < 0, offset + total, offset)
        here = offset < KVH * pages
        group = jnp.zeros((1, HD), jnp.int32)
        for g in range(1, KVH):
            group = group + (offset >= g * pages).astype(jnp.int32)
        pair = jnp.where(here, r * KVH + group, pair)
        alive = jnp.where(here, lengths[r] - 1 - (offset - group * pages) * PAGE, alive)
    pair_of[...] = pair
    live[...] = alive


def prepare_kernel(
    device, lengths, table, near, tables, own_tables, pair_of, live, square, *, slots
):
    chips, requests, _ = near.shape
    total = jnp.zeros(square.shape, f32)
    for chip in range(chips):
        values = near[chip].astype(f32)
        total = total + values * values
    square[...] = total
    row, lane = lax.broadcasted_iota(jnp.int32, (requests, HD), 0), lane_of((requests, HD))
    position = jnp.zeros((requests, HD), f32)
    for r in range(requests):
        position = jnp.where(row == r, (lengths[r] - 1).astype(f32), position)
    index = jnp.where(lane < HALF, lane, lane - HALF).astype(f32)
    angles = position * jnp.exp(index * (-2.0 * math.log(rope_base) / HD))
    sine = jnp.sin(angles)
    tables[:requests] = jnp.cos(angles)
    tables[requests:] = jnp.where(lane < HALF, -sine, sine)
    mine = lax.div(device[0], 2)
    keys_here = lax.rem(device[0], 2) == 0
    own_tables[0:1, :] = jnp.where(keys_here, tables[pl.ds(mine, 1), :], 1.0)
    own_tables[1:2, :] = jnp.where(keys_here, tables[pl.ds(requests + mine, 1), :], 0.0)
    place_slots(device[0], lengths, table, pair_of, live, slots, 2 * chips * slots)


def normalize_kernel(device, near, far, square, gain, w_kv, normed, kept, away):
    chips, requests, width = near.shape
    n = 2 * chips
    core = lax.rem(device[0], 2)
    total = square[...]
    for chip in range(chips):
        values = far[chip].astype(f32)
        total = total + values * values
    scale = lax.rsqrt(jnp.sum(total, axis=1, keepdims=True) / (n * width) + 1e-05)
    for k in range(n):
        chip, from_core = divmod(k, 2)
        values = jnp.where(core == from_core, near[chip].astype(f32), far[chip].astype(f32))
        normed[k] = (values * scale * gain[:, k * width : (k + 1) * width]).astype(bf16)
    own = normed[device[0]]
    for result, half in ((kept, core), (away, 1 - core)):
        columns = pl.ds(pl.multiple_of(half * KV, KV), KV)
        result[...] = jnp.dot(own, w_kv[:, columns], preferred_element_type=f32)


def query_kernel(normed, tables, w_query, query):
    n, requests, width = normed.shape
    columns = w_query.shape[1]
    product = jnp.zeros((requests, columns), f32)
    for k in range(n):
        product = product + jnp.dot(
            normed[k], w_query[k * width : (k + 1) * width, :], preferred_element_type=f32
        )
    cosine, sine = tables[:requests], tables[requests:]
    for c in range(columns // HD):
        turned = rotate(product[:, c * HD : (c + 1) * HD], cosine, sine)
        query[:, c * HD : (c + 1) * HD] = turned.astype(bf16)


def gather_kernel(query, kept, came, send, kv_rows):
    chips, requests, wide = send.shape
    columns = wide - HD
    for group in range(KVH):
        part = slice(group * HD, (group + 1) * HD)
        value = kept[:, part] + came[:, part]
        upper = value.astype(bf16).astype(f32)
        kv_rows[pl.ds(group, requests, stride=2 * KVH), :] = upper
        kv_rows[pl.ds(KVH + group, requests, stride=2 * KVH), :] = value - upper
    whole = query[...]
    for chip in range(chips):
        send[chip, :, :columns] = whole
        rows = kv_rows[chip * 2 * KVH : (chip + 1) * 2 * KVH, :]
        if requests > 2 * KVH:
            rows = jnp.concatenate([rows, jnp.zeros((requests - 2 * KVH, HD), f32)], axis=0)
        send[chip, :, columns:] = rows.astype(bf16)


def entry_kernel(got, own_tables, row):
    columns = got.shape[2] - HD
    kv = jnp.zeros((2 * KVH, HD), f32)
    for chip in range(got.shape[0]):
        kv = kv + got[chip, : 2 * KVH, columns:].astype(f32)
    kv = kv + pltpu.roll(kv, KVH, 0)
    row[...] = rotate(kv, own_tables[0:1, :], own_tables[1:2, :]).astype(bf16)


def attend_kernel(
    pair_of, live, got, k_near, v_near, k_far, v_far, peak, total, mixed,
    queries, slot_score, slot_out, slot_peak, slot_total, run_peak, run_total, run_mixed,
):
    chips, requests, wide = got.shape
    heads = (wide - HD) // HD
    slots, page = k_near.shape[:2]
    pairs = requests * KVH
    for h in range(CORE_H):
        chip, c = divmod(h, heads)
        queries[pl.ds(h, requests, stride=CORE_H), :] = got[
            chip, :, c * HD : (c + 1) * HD
        ].astype(f32)
    queries[pairs * CORE_GH :, :] = jnp.zeros((CORE_GH, HD), f32)
    run_peak[...] = jnp.full_like(run_peak, lowest)
    run_total[...] = jnp.zeros_like(run_total)
    run_mixed[...] = jnp.zeros_like(run_mixed)

    def rows_of(s, side=0):
        start = (pair_of[0, s] + side * (pairs + 1)) * CORE_GH
        return pl.ds(pl.multiple_of(start, CORE_GH), CORE_GH)

    for s in range(0, 2 * slots, 2):
        pages, at = (k_near, s) if s < slots else (k_far, s - slots)
        both = jnp.concatenate([queries[rows_of(s), :], queries[rows_of(s + 1), :]], axis=0)
        scores = lax.dot_general(
            both.astype(bf16), pages[at : at + 2].reshape(2 * page, HD), (((1,), (1,)), ((), ())),
            preferred_element_type=f32,
        )
        slot_score[s] = scores[:CORE_GH, :page]
        slot_score[s + 1] = scores[CORE_GH:, page:]
    shape = (CORE_GH, HD)
    places = lane_of((CORE_GH, page))
    for s in range(2 * slots):
        alive = places < live[0, s]
        scores = jnp.where(alive, slot_score[s] * score_scale, lowest)
        top = jnp.max(scores, axis=1, keepdims=True)
        weights = jnp.where(alive, jnp.exp(scores - top), 0.0)
        slot_score[s] = weights
        slot_peak[s] = jnp.broadcast_to(top, shape)
        slot_total[s] = jnp.broadcast_to(jnp.sum(weights, axis=1, keepdims=True), shape)
    nothing = jnp.zeros((CORE_GH, page), f32)
    for s in range(0, 2 * slots, 2):
        pages, at = (v_near, s) if s < slots else (v_far, s - slots)
        upper = jnp.concatenate([slot_score[s], nothing], axis=1)
        lower = jnp.concatenate([nothing, slot_score[s + 1]], axis=1)
        both = jnp.concatenate([upper, lower], axis=0).astype(bf16)
        out = jnp.dot(
            both, pages[at : at + 2].reshape(2 * page, HD), preferred_element_type=f32
        )
        slot_out[s] = out[:CORE_GH]
        slot_out[s + 1] = out[CORE_GH:]
    running = [jnp.full(shape, lowest, f32)] * 2
    for t in range(slots):
        for side in range(2):
            s = side * slots + t
            if t:
                same = pair_of[0, s] == pair_of[0, s - 1]
                running[side] = jnp.where(same, running[side], lowest)
            running[side] = jnp.maximum(slot_peak[s], running[side])
            run_peak[rows_of(s, side), :] = running[side]
    for s in range(2 * slots):
        slot_peak[s] = jnp.exp(slot_peak[s] - run_peak[rows_of(s, s // slots), :])
    sum_total = [jnp.zeros(shape, f32)] * 2
    sum_mixed = [jnp.zeros(shape, f32)] * 2
    for t in range(slots):
        for side in range(2):
            s = side * slots + t
            if t:
                keep = jnp.where(pair_of[0, s] == pair_of[0, s - 1], 1.0, 0.0)
                sum_total[side], sum_mixed[side] = keep * sum_total[side], keep * sum_mixed[side]
            rows, factor = rows_of(s, side), slot_peak[s]
            sum_total[side] = sum_total[side] + factor * slot_total[s]
            sum_mixed[side] = sum_mixed[side] + factor * slot_out[s]
            run_total[rows, :] = sum_total[side]
            run_mixed[rows, :] = sum_mixed[side]
    for pair in range(pairs):
        here = slice(pair * CORE_GH, (pair + 1) * CORE_GH)
        first = run_peak[here, :]
        there = slice((pairs + 1 + pair) * CORE_GH, (pairs + 2 + pair) * CORE_GH)
        second = run_peak[there, :]
        top = jnp.maximum(first, second)
        first, second = jnp.exp(first - top), jnp.exp(second - top)
        peak[here, :] = top
        total[here, :] = first * run_total[here, :] + second * run_total[there, :]
        mixed[here, :] = first * run_mixed[here, :] + second * run_mixed[there, :]


def share_kernel(device, peak, total, mixed, near_row, far_row, send, kv_block):
    chips, requests, wide = send.shape
    columns = wide - 2 * HD
    heads = columns // HD
    core = lax.rem(device[0], 2)
    near, far = near_row[...].astype(f32), far_row[...].astype(f32)
    keys_here = lax.broadcasted_iota(jnp.int32, near.shape, 0) < KVH
    own = jnp.where(core == 0, near, far)
    other = jnp.where(core == 0, far, near)
    if requests > 2 * KVH:
        kv_block[...] = jnp.zeros_like(kv_block)
    kv_block[: 2 * KVH, :] = jnp.where(keys_here, own, other)
    lanes = lane_of((requests, HD))
    order = lax.rem(lanes, heads)
    kind = lax.div(lanes, heads)
    kinds = lax.rem(kind, 3)
    for chip in range(chips):
        stats = jnp.zeros((requests, HD), f32)
        for c in range(heads):
            rows = pl.ds(chip * heads + c, requests, stride=CORE_H)
            send[chip, :, c * HD : (c + 1) * HD] = mixed[rows, :].astype(bf16)
            value = jnp.where(kind < 3, peak[rows, :], total[rows, :])
            stats = jnp.where(order == c, value, stats)
        first = stats.astype(bf16).astype(f32)
        stats = stats - first
        second = stats.astype(bf16).astype(f32)
        third = stats - second
        stats = jnp.where(kinds == 0, first, jnp.where(kinds == 1, second, third))
        send[chip, :, columns : columns + HD] = stats.astype(bf16)
        send[chip, :, columns + HD :] = kv_block[...].astype(bf16)


def multiply_out(attention, w_out, result, core):
    chips, _, width = result.shape
    whole = attention[...]
    for chip in range(chips):
        columns = pl.ds(pl.multiple_of((2 * chip + core) * width, HD), width)
        result[chip] = jnp.dot(
            whole, w_out[:, columns], preferred_element_type=f32
        ).astype(result.dtype)


def combine_kernel(device, got, query, w_out, away, attention, entries):
    chips, requests, wide = got.shape
    columns = wide - 2 * HD
    heads = columns // HD
    lanes = lane_of((requests, HD))
    for request in range(requests):
        block = got[request, : 2 * KVH, columns + HD :].astype(f32)
        entries[pl.ds(request, 2 * KVH, stride=requests), :] = block

    def own(c, half):
        start = (lax.div(device[0] * heads + c, GH) + half * KVH) * requests
        return entries[pl.ds(pl.multiple_of(start, 8), requests), :]

    new_score = jnp.full((requests, HD), lowest, f32)
    for c in range(heads):
        score = query[:, c * HD : (c + 1) * HD].astype(f32) * own(c, 0)
        score = jnp.sum(score, axis=1, keepdims=True) * score_scale
        new_score = jnp.where(lanes == c, score, new_score)
    peaks, totals = [], []
    for src in range(chips):
        stats = got[src, :, columns : columns + HD].astype(f32)
        stats = (
            stats + pltpu.roll(stats, HD - heads, 1) + pltpu.roll(stats, HD - 2 * heads, 1)
        )
        peaks.append(stats)
        totals.append(pltpu.roll(stats, HD - 3 * heads, 1))
    top = new_score
    for value in peaks:
        top = jnp.maximum(top, value)
    weights = [jnp.exp(value - top) for value in peaks]
    new_weight = jnp.exp(new_score - top)
    total = new_weight
    for weight, value in zip(weights, totals):
        total = total + weight * value
    inverse = 1.0 / total
    weights = [weight * inverse for weight in weights]
    new_weight = new_weight * inverse
    for c in range(heads):
        mixed = new_weight[:, c : c + 1] * own(c, 1)
        for src in range(chips):
            mixed = mixed + weights[src][:, c : c + 1] * got[
                src, :, c * HD : (c + 1) * HD
            ].astype(f32)
        attention[:, c * HD : (c + 1) * HD] = mixed.astype(bf16)
    multiply_out(attention, w_out, away, 1 - lax.rem(device[0], 2))


def keep_kernel(device, attention, w_out, kept):
    multiply_out(attention, w_out, kept, lax.rem(device[0], 2))


def join_kernel(kept, came, send):
    for chip in range(send.shape[0]):
        send[chip] = (kept[chip] + came[chip].astype(f32)).astype(bf16)


def call(kernel, out_shape, in_spaces, out_spaces, scratch, limit, moved=None):
    return pl.pallas_call(
        kernel,
        out_shape=out_shape,
        in_specs=[pl.BlockSpec(memory_space=space) for space in in_spaces],
        out_specs=[pl.BlockSpec(memory_space=space) for space in out_spaces],
        scratch_shapes=scratch,
        compiler_params=pltpu.CompilerParams(vmem_limit_bytes=limit << 20),
        cost_estimate=moved
        and pl.CostEstimate(flops=moved * 512, bytes_accessed=moved, transcendentals=0),
    )


def local(hidden, gain, w_query, w_kv, w_out, k_cache, v_cache, block_table, lengths):
    device = lax.axis_index("attn").astype(jnp.int32).reshape(1)
    n = lax.axis_size("attn")
    requests, width = hidden.shape
    columns = w_query.shape[1]
    slots = k_cache.shape[0]
    pairs = requests * KVH
    assert 2 * requests == n and slots % 2 == 0 and 2 * slots <= HD

    shape = jax.ShapeDtypeStruct
    halves = shape((n // 2, requests, width), bf16)
    device, k_cache, v_cache = lax.optimization_barrier((device, k_cache, v_cache))
    k_far, v_far = swap_cores(k_cache), swap_cores(v_cache)
    (send,) = call(
        spread_kernel,
        [halves],
        [SMEM, VMEM],
        [VMEM],
        [],
        2,
        2 * (w_query.nbytes + w_kv.nbytes),
    )(device, hidden)
    near = exchange(send)
    far = swap_cores(near)
    tables, own_tables, pair_of, live, square = call(
        functools.partial(prepare_kernel, slots=slots),
        [
            shape((2 * requests, HD), f32),
            shape((2, HD), f32),
            shape((1, HD), jnp.int32),
            shape((1, HD), jnp.int32),
            shape((requests, width), f32),
        ],
        [SMEM] * 3 + [VMEM],
        [VMEM] * 5,
        [],
        2,
    )(device, lengths, block_table, near)
    half_kv = shape((requests, KV), f32)
    normed, kept, away = call(
        normalize_kernel,
        [shape((n, requests, width), bf16), half_kv, half_kv],
        [SMEM] + [VMEM] * 5,
        [VMEM] * 3,
        [],
        4,
    )(device, near, far, square, gain.reshape(1, n * width), w_kv)
    came = swap_cores(away)
    (query,) = call(
        query_kernel, [shape((requests, columns), bf16)], [VMEM] * 3, [VMEM], [], 4
    )(normed, tables, w_query)
    (send,) = call(
        gather_kernel,
        [shape((n // 2, requests, columns + HD), bf16)],
        [VMEM] * 3,
        [VMEM],
        [pltpu.VMEM((requests * 2 * KVH, HD), f32)],
        4,
    )(query, kept, came)
    got = exchange(send)
    (near_row,) = call(entry_kernel, [shape((2 * KVH, HD), bf16)], [VMEM] * 2, [VMEM], [], 2)(
        got, own_tables
    )
    far_row = swap_cores(near_row)
    rows = shape((pairs * CORE_GH, HD), f32)
    slot_rows = pltpu.VMEM((2 * slots, CORE_GH, HD), f32)
    run_rows = pltpu.VMEM((2 * (pairs + 1) * CORE_GH, HD), f32)
    peak, total, mixed = call(
        attend_kernel,
        [rows] * 3,
        [SMEM] * 2 + [VMEM] * 5,
        [VMEM] * 3,
        [pltpu.VMEM(((pairs + 1) * CORE_GH, HD), f32)] + [slot_rows] * 4 + [run_rows] * 3,
        8,
    )(pair_of, live, got, k_cache, v_cache, k_far, v_far)
    (send,) = call(
        share_kernel,
        [shape((n // 2, requests, columns + 2 * HD), bf16)],
        [SMEM] + [VMEM] * 5,
        [VMEM],
        [pltpu.VMEM((requests, HD), f32)],
        4,
    )(device, peak, total, mixed, near_row, far_row)
    got = exchange(send)
    away, attention, entries = call(
        combine_kernel,
        [
            halves,
            shape((requests, columns), bf16),
            shape((2 * KVH * requests, HD), f32),
        ],
        [SMEM] + [VMEM] * 3,
        [VMEM] * 3,
        [],
        4,
    )(device, got, query, w_out)
    came = swap_cores(away)
    (kept,) = call(
        keep_kernel, [shape(halves.shape, f32)], [SMEM] + [VMEM] * 2, [VMEM], [], 4
    )(device, attention, w_out)
    (send,) = call(join_kernel, [halves], [VMEM] * 2, [VMEM], [], 4)(kept, came)
    got = exchange(send)
    attn_out, new_entries = call(
        add_kernel,
        [shape((requests, width), bf16), shape((requests, 2 * KV), bf16)],
        [VMEM] * 2,
        [VMEM] * 2,
        [],
        4,
    )(got, entries)
    return attn_out, new_entries


def solution(mesh):
    in_specs = (
        P("groups", "attn"),
        P(),
        P(None, "attn"),
        P("attn", None),
        P("attn", None),
        P(("groups", "attn"), None, None),
        P(("groups", "attn"), None, None),
        P("groups", None, None),
        P("groups"),
    )
    out_specs = (P("groups", "attn"), P("groups", None))
    return jax.shard_map(local, mesh=mesh, in_specs=in_specs, out_specs=out_specs, check_vma=False)
```

```python
import functools
import math

import jax
import jax.numpy as jnp
from jax import lax
from jax.experimental import pallas as pl
from jax.experimental.pallas import tpu as pltpu
from jax.sharding import PartitionSpec as P

HD = 128
H = 64
KVH = 4
GH = H // KVH
CORE_H = H // 2
CORE_GH = GH // 2

lowest = -1e30
rope_base = 500000.0
score_scale = 1.0 / math.sqrt(HD)
bf16 = jnp.bfloat16
f32 = jnp.float32
VMEM = pltpu.MemorySpace.VMEM
SMEM = pltpu.MemorySpace.SMEM
KV = KVH * HD
PAGE = 128
HALF = HD // 2


def rotate(vectors, cosine, sine):
    return vectors * cosine + pltpu.roll(vectors, HALF, 1) * sine


def exchange(buffer):
    chips = buffer.shape[0]
    groups = [[2 * chip + core for chip in range(chips)] for core in range(2)]
    return lax.all_to_all(buffer, "attn", 0, 0, tiled=True, axis_index_groups=groups)


def swap_cores(buffer):
    n = lax.axis_size("attn")
    return lax.ppermute(buffer, "attn", [(i, i ^ 1) for i in range(n)])


def lane_of(shape):
    return lax.broadcasted_iota(jnp.int32, shape, 1)


def spread_kernel(device, hidden, send):
    for j in range(send.shape[0]):
        send[j] = hidden[...]


def add_kernel(got, entries, out, new_entries):
    total = got[0].astype(f32)
    for src in range(1, got.shape[0]):
        total = total + got[src].astype(f32)
    out[...] = total.astype(bf16)
    requests = out.shape[0]
    for i in range(2 * KVH):
        rows = slice(i * requests, (i + 1) * requests)
        new_entries[:, i * HD : (i + 1) * HD] = entries[rows, :].astype(bf16)


def place_slots(device, lengths, table, pair_of, live, slots, total):
    requests = table.shape[0]
    lane = lane_of((1, HD))
    partner = device + 1 - 2 * lax.rem(device, 2)
    slot = jnp.where(lane < slots, device * slots + lane, (partner - 1) * slots + lane)
    pair = jnp.full((1, HD), requests * KVH, jnp.int32)
    alive = jnp.zeros((1, HD), jnp.int32)
    for r in range(requests):
        pages = lax.div(lengths[r] + PAGE - 1, PAGE)
        offset = slot - table[r, 0, 0]
        offset = jnp.where(offset < 0, offset + total, offset)
        here = offset < KVH * pages
        group = jnp.zeros((1, HD), jnp.int32)
        for g in range(1, KVH):
            group = group + (offset >= g * pages).astype(jnp.int32)
        pair = jnp.where(here, r * KVH + group, pair)
        alive = jnp.where(here, lengths[r] - 1 - (offset - group * pages) * PAGE, alive)
    pair_of[...] = pair
    live[...] = alive


def prepare_kernel(
    device, lengths, table, near, tables, own_tables, pair_of, live, square, *, slots
):
    chips, requests, _ = near.shape
    total = jnp.zeros(square.shape, f32)
    for chip in range(chips):
        values = near[chip].astype(f32)
        total = total + values * values
    square[...] = total
    row, lane = lax.broadcasted_iota(jnp.int32, (requests, HD), 0), lane_of((requests, HD))
    position = jnp.zeros((requests, HD), f32)
    for r in range(requests):
        position = jnp.where(row == r, (lengths[r] - 1).astype(f32), position)
    index = jnp.where(lane < HALF, lane, lane - HALF).astype(f32)
    angles = position * jnp.exp(index * (-2.0 * math.log(rope_base) / HD))
    sine = jnp.sin(angles)
    tables[:requests] = jnp.cos(angles)
    tables[requests:] = jnp.where(lane < HALF, -sine, sine)
    mine = lax.div(device[0], 2)
    keys_here = lax.rem(device[0], 2) == 0
    own_tables[0:1, :] = jnp.where(keys_here, tables[pl.ds(mine, 1), :], 1.0)
    own_tables[1:2, :] = jnp.where(keys_here, tables[pl.ds(requests + mine, 1), :], 0.0)
    place_slots(device[0], lengths, table, pair_of, live, slots, 2 * chips * slots)


def normalize_kernel(device, near, far, square, gain, w_kv, normed, kept, away):
    chips, requests, width = near.shape
    n = 2 * chips
    core = lax.rem(device[0], 2)
    total = square[...]
    for chip in range(chips):
        values = far[chip].astype(f32)
        total = total + values * values
    scale = lax.rsqrt(jnp.sum(total, axis=1, keepdims=True) / (n * width) + 1e-05)
    for k in range(n):
        chip, from_core = divmod(k, 2)
        values = jnp.where(core == from_core, near[chip].astype(f32), far[chip].astype(f32))
        normed[k] = (values * scale * gain[:, k * width : (k + 1) * width]).astype(bf16)
    own = normed[device[0]]
    for result, half in ((kept, core), (away, 1 - core)):
        columns = pl.ds(pl.multiple_of(half * KV, KV), KV)
        result[...] = jnp.dot(own, w_kv[:, columns], preferred_element_type=f32)


def query_kernel(normed, tables, w_query, query):
    n, requests, width = normed.shape
    columns = w_query.shape[1]
    product = jnp.zeros((requests, columns), f32)
    for k in range(n):
        product = product + jnp.dot(
            normed[k], w_query[k * width : (k + 1) * width, :], preferred_element_type=f32
        )
    cosine, sine = tables[:requests], tables[requests:]
    for c in range(columns // HD):
        turned = rotate(product[:, c * HD : (c + 1) * HD], cosine, sine)
        query[:, c * HD : (c + 1) * HD] = turned.astype(bf16)


def gather_kernel(query, kept, came, send, kv_rows):
    chips, requests, wide = send.shape
    columns = wide - HD
    for group in range(KVH):
        part = slice(group * HD, (group + 1) * HD)
        value = kept[:, part] + came[:, part]
        upper = value.astype(bf16).astype(f32)
        kv_rows[pl.ds(group, requests, stride=2 * KVH), :] = upper
        kv_rows[pl.ds(KVH + group, requests, stride=2 * KVH), :] = value - upper
    whole = query[...]
    for chip in range(chips):
        send[chip, :, :columns] = whole
        rows = kv_rows[chip * 2 * KVH : (chip + 1) * 2 * KVH, :]
        if requests > 2 * KVH:
            rows = jnp.concatenate([rows, jnp.zeros((requests - 2 * KVH, HD), f32)], axis=0)
        send[chip, :, columns:] = rows.astype(bf16)


def entry_kernel(got, own_tables, row):
    columns = got.shape[2] - HD
    kv = jnp.zeros((2 * KVH, HD), f32)
    for chip in range(got.shape[0]):
        kv = kv + got[chip, : 2 * KVH, columns:].astype(f32)
    kv = kv + pltpu.roll(kv, KVH, 0)
    row[...] = rotate(kv, own_tables[0:1, :], own_tables[1:2, :]).astype(bf16)


def attend_kernel(
    pair_of, live, got, k_near, v_near, k_far, v_far, peak, total, mixed,
    queries, slot_score, slot_out, slot_peak, slot_total, run_peak, run_total, run_mixed,
):
    chips, requests, wide = got.shape
    heads = (wide - HD) // HD
    slots, page = k_near.shape[:2]
    pairs = requests * KVH
    for h in range(CORE_H):
        chip, c = divmod(h, heads)
        queries[pl.ds(h, requests, stride=CORE_H), :] = got[
            chip, :, c * HD : (c + 1) * HD
        ].astype(f32)
    queries[pairs * CORE_GH :, :] = jnp.zeros((CORE_GH, HD), f32)
    run_peak[...] = jnp.full_like(run_peak, lowest)
    run_total[...] = jnp.zeros_like(run_total)
    run_mixed[...] = jnp.zeros_like(run_mixed)

    def rows_of(s, side=0):
        start = (pair_of[0, s] + side * (pairs + 1)) * CORE_GH
        return pl.ds(pl.multiple_of(start, CORE_GH), CORE_GH)

    for s in range(0, 2 * slots, 2):
        pages, at = (k_near, s) if s < slots else (k_far, s - slots)
        both = jnp.concatenate([queries[rows_of(s), :], queries[rows_of(s + 1), :]], axis=0)
        scores = lax.dot_general(
            both.astype(bf16), pages[at : at + 2].reshape(2 * page, HD), (((1,), (1,)), ((), ())),
            preferred_element_type=f32,
        )
        slot_score[s] = scores[:CORE_GH, :page]
        slot_score[s + 1] = scores[CORE_GH:, page:]
    shape = (CORE_GH, HD)
    places = lane_of((CORE_GH, page))
    for s in range(2 * slots):
        alive = places < live[0, s]
        scores = jnp.where(alive, slot_score[s] * score_scale, lowest)
        top = jnp.max(scores, axis=1, keepdims=True)
        weights = jnp.where(alive, jnp.exp(scores - top), 0.0)
        slot_score[s] = weights
        slot_peak[s] = jnp.broadcast_to(top, shape)
        slot_total[s] = jnp.broadcast_to(jnp.sum(weights, axis=1, keepdims=True), shape)
    nothing = jnp.zeros((CORE_GH, page), f32)
    for s in range(0, 2 * slots, 2):
        pages, at = (v_near, s) if s < slots else (v_far, s - slots)
        upper = jnp.concatenate([slot_score[s], nothing], axis=1)
        lower = jnp.concatenate([nothing, slot_score[s + 1]], axis=1)
        both = jnp.concatenate([upper, lower], axis=0).astype(bf16)
        out = jnp.dot(
            both, pages[at : at + 2].reshape(2 * page, HD), preferred_element_type=f32
        )
        slot_out[s] = out[:CORE_GH]
        slot_out[s + 1] = out[CORE_GH:]
    running = [jnp.full(shape, lowest, f32)] * 2
    for t in range(slots):
        for side in range(2):
            s = side * slots + t
            if t:
                same = pair_of[0, s] == pair_of[0, s - 1]
                running[side] = jnp.where(same, running[side], lowest)
            running[side] = jnp.maximum(slot_peak[s], running[side])
            run_peak[rows_of(s, side), :] = running[side]
    for s in range(2 * slots):
        slot_peak[s] = jnp.exp(slot_peak[s] - run_peak[rows_of(s, s // slots), :])
    sum_total = [jnp.zeros(shape, f32)] * 2
    sum_mixed = [jnp.zeros(shape, f32)] * 2
    for t in range(slots):
        for side in range(2):
            s = side * slots + t
            if t:
                keep = jnp.where(pair_of[0, s] == pair_of[0, s - 1], 1.0, 0.0)
                sum_total[side], sum_mixed[side] = keep * sum_total[side], keep * sum_mixed[side]
            rows, factor = rows_of(s, side), slot_peak[s]
            sum_total[side] = sum_total[side] + factor * slot_total[s]
            sum_mixed[side] = sum_mixed[side] + factor * slot_out[s]
            run_total[rows, :] = sum_total[side]
            run_mixed[rows, :] = sum_mixed[side]
    for pair in range(pairs):
        here = slice(pair * CORE_GH, (pair + 1) * CORE_GH)
        first = run_peak[here, :]
        there = slice((pairs + 1 + pair) * CORE_GH, (pairs + 2 + pair) * CORE_GH)
        second = run_peak[there, :]
        top = jnp.maximum(first, second)
        first, second = jnp.exp(first - top), jnp.exp(second - top)
        peak[here, :] = top
        total[here, :] = first * run_total[here, :] + second * run_total[there, :]
        mixed[here, :] = first * run_mixed[here, :] + second * run_mixed[there, :]


def share_kernel(device, peak, total, mixed, near_row, far_row, send, kv_block):
    chips, requests, wide = send.shape
    columns = wide - 2 * HD
    heads = columns // HD
    core = lax.rem(device[0], 2)
    near, far = near_row[...].astype(f32), far_row[...].astype(f32)
    keys_here = lax.broadcasted_iota(jnp.int32, near.shape, 0) < KVH
    own = jnp.where(core == 0, near, far)
    other = jnp.where(core == 0, far, near)
    if requests > 2 * KVH:
        kv_block[...] = jnp.zeros_like(kv_block)
    kv_block[: 2 * KVH, :] = jnp.where(keys_here, own, other)
    lanes = lane_of((requests, HD))
    order = lax.rem(lanes, heads)
    kind = lax.div(lanes, heads)
    kinds = lax.rem(kind, 3)
    for chip in range(chips):
        stats = jnp.zeros((requests, HD), f32)
        for c in range(heads):
            rows = pl.ds(chip * heads + c, requests, stride=CORE_H)
            send[chip, :, c * HD : (c + 1) * HD] = mixed[rows, :].astype(bf16)
            value = jnp.where(kind < 3, peak[rows, :], total[rows, :])
            stats = jnp.where(order == c, value, stats)
        first = stats.astype(bf16).astype(f32)
        stats = stats - first
        second = stats.astype(bf16).astype(f32)
        third = stats - second
        stats = jnp.where(kinds == 0, first, jnp.where(kinds == 1, second, third))
        send[chip, :, columns : columns + HD] = stats.astype(bf16)
        send[chip, :, columns + HD :] = kv_block[...].astype(bf16)


def multiply_out(attention, w_out, result, core):
    chips, _, width = result.shape
    whole = attention[...]
    for chip in range(chips):
        columns = pl.ds(pl.multiple_of((2 * chip + core) * width, HD), width)
        result[chip] = jnp.dot(
            whole, w_out[:, columns], preferred_element_type=f32
        ).astype(result.dtype)


def combine_kernel(device, got, query, w_out, away, attention, entries):
    chips, requests, wide = got.shape
    columns = wide - 2 * HD
    heads = columns // HD
    lanes = lane_of((requests, HD))
    for request in range(requests):
        block = got[request, : 2 * KVH, columns + HD :].astype(f32)
        entries[pl.ds(request, 2 * KVH, stride=requests), :] = block

    def own(c, half):
        start = (lax.div(device[0] * heads + c, GH) + half * KVH) * requests
        return entries[pl.ds(pl.multiple_of(start, 8), requests), :]

    new_score = jnp.full((requests, HD), lowest, f32)
    for c in range(heads):
        score = query[:, c * HD : (c + 1) * HD].astype(f32) * own(c, 0)
        score = jnp.sum(score, axis=1, keepdims=True) * score_scale
        new_score = jnp.where(lanes == c, score, new_score)
    peaks, totals = [], []
    for src in range(chips):
        stats = got[src, :, columns : columns + HD].astype(f32)
        stats = (
            stats + pltpu.roll(stats, HD - heads, 1) + pltpu.roll(stats, HD - 2 * heads, 1)
        )
        peaks.append(stats)
        totals.append(pltpu.roll(stats, HD - 3 * heads, 1))
    top = new_score
    for value in peaks:
        top = jnp.maximum(top, value)
    weights = [jnp.exp(value - top) for value in peaks]
    new_weight = jnp.exp(new_score - top)
    total = new_weight
    for weight, value in zip(weights, totals):
        total = total + weight * value
    inverse = 1.0 / total
    weights = [weight * inverse for weight in weights]
    new_weight = new_weight * inverse
    for c in range(heads):
        mixed = new_weight[:, c : c + 1] * own(c, 1)
        for src in range(chips):
            mixed = mixed + weights[src][:, c : c + 1] * got[
                src, :, c * HD : (c + 1) * HD
            ].astype(f32)
        attention[:, c * HD : (c + 1) * HD] = mixed.astype(bf16)
    multiply_out(attention, w_out, away, 1 - lax.rem(device[0], 2))


def keep_kernel(device, attention, w_out, kept):
    multiply_out(attention, w_out, kept, lax.rem(device[0], 2))


def join_kernel(kept, came, send):
    for chip in range(send.shape[0]):
        send[chip] = (kept[chip] + came[chip].astype(f32)).astype(bf16)


def call(kernel, out_shape, in_spaces, out_spaces, scratch, limit, moved=None):
    return pl.pallas_call(
        kernel,
        out_shape=out_shape,
        in_specs=[pl.BlockSpec(memory_space=space) for space in in_spaces],
        out_specs=[pl.BlockSpec(memory_space=space) for space in out_spaces],
        scratch_shapes=scratch,
        compiler_params=pltpu.CompilerParams(vmem_limit_bytes=limit << 20),
        cost_estimate=moved
        and pl.CostEstimate(flops=moved * 512, bytes_accessed=moved, transcendentals=0),
    )


def local(hidden, gain, w_query, w_kv, w_out, k_cache, v_cache, block_table, lengths):
    device = lax.axis_index("attn").astype(jnp.int32).reshape(1)
    n = lax.axis_size("attn")
    requests, width = hidden.shape
    columns = w_query.shape[1]
    slots = k_cache.shape[0]
    pairs = requests * KVH
    assert 2 * requests == n and slots % 2 == 0 and 2 * slots <= HD

    shape = jax.ShapeDtypeStruct
    halves = shape((n // 2, requests, width), bf16)
    (send,) = call(
        spread_kernel,
        [halves],
        [SMEM, VMEM],
        [VMEM],
        [],
        2,
        2 * (w_query.nbytes + w_kv.nbytes),
    )(device, hidden)
    near = exchange(send)
    far = swap_cores(near)
    tables, own_tables, pair_of, live, square = call(
        functools.partial(prepare_kernel, slots=slots),
        [
            shape((2 * requests, HD), f32),
            shape((2, HD), f32),
            shape((1, HD), jnp.int32),
            shape((1, HD), jnp.int32),
            shape((requests, width), f32),
        ],
        [SMEM] * 3 + [VMEM],
        [VMEM] * 5,
        [],
        2,
    )(device, lengths, block_table, near)
    half_kv = shape((requests, KV), f32)
    normed, kept, away = call(
        normalize_kernel,
        [shape((n, requests, width), bf16), half_kv, half_kv],
        [SMEM] + [VMEM] * 5,
        [VMEM] * 3,
        [],
        4,
    )(device, near, far, square, gain.reshape(1, n * width), w_kv)
    came = swap_cores(away)
    (query,) = call(
        query_kernel, [shape((requests, columns), bf16)], [VMEM] * 3, [VMEM], [], 4
    )(normed, tables, w_query)
    (send,) = call(
        gather_kernel,
        [shape((n // 2, requests, columns + HD), bf16)],
        [VMEM] * 3,
        [VMEM],
        [pltpu.VMEM((requests * 2 * KVH, HD), f32)],
        4,
    )(query, kept, came)
    send, k_cache, v_cache = lax.optimization_barrier((send, k_cache, v_cache))
    k_far, v_far = swap_cores(k_cache), swap_cores(v_cache)
    got = exchange(send)
    (near_row,) = call(entry_kernel, [shape((2 * KVH, HD), bf16)], [VMEM] * 2, [VMEM], [], 2)(
        got, own_tables
    )
    far_row = swap_cores(near_row)
    rows = shape((pairs * CORE_GH, HD), f32)
    slot_rows = pltpu.VMEM((2 * slots, CORE_GH, HD), f32)
    run_rows = pltpu.VMEM((2 * (pairs + 1) * CORE_GH, HD), f32)
    peak, total, mixed = call(
        attend_kernel,
        [rows] * 3,
        [SMEM] * 2 + [VMEM] * 5,
        [VMEM] * 3,
        [pltpu.VMEM(((pairs + 1) * CORE_GH, HD), f32)] + [slot_rows] * 4 + [run_rows] * 3,
        8,
    )(pair_of, live, got, k_cache, v_cache, k_far, v_far)
    (send,) = call(
        share_kernel,
        [shape((n // 2, requests, columns + 2 * HD), bf16)],
        [SMEM] + [VMEM] * 5,
        [VMEM],
        [pltpu.VMEM((requests, HD), f32)],
        4,
    )(device, peak, total, mixed, near_row, far_row)
    got = exchange(send)
    away, attention, entries = call(
        combine_kernel,
        [
            halves,
            shape((requests, columns), bf16),
            shape((2 * KVH * requests, HD), f32),
        ],
        [SMEM] + [VMEM] * 3,
        [VMEM] * 3,
        [],
        4,
    )(device, got, query, w_out)
    came = swap_cores(away)
    (kept,) = call(
        keep_kernel, [shape(halves.shape, f32)], [SMEM] + [VMEM] * 2, [VMEM], [], 4
    )(device, attention, w_out)
    (send,) = call(join_kernel, [halves], [VMEM] * 2, [VMEM], [], 4)(kept, came)
    got = exchange(send)
    attn_out, new_entries = call(
        add_kernel,
        [shape((requests, width), bf16), shape((requests, 2 * KV), bf16)],
        [VMEM] * 2,
        [VMEM] * 2,
        [],
        4,
    )(got, entries)
    return attn_out, new_entries


def solution(mesh):
    in_specs = (
        P("groups", "attn"),
        P(),
        P(None, "attn"),
        P("attn", None),
        P("attn", None),
        P(("groups", "attn"), None, None),
        P(("groups", "attn"), None, None),
        P("groups", None, None),
        P("groups"),
    )
    out_specs = (P("groups", "attn"), P("groups", None))
    return jax.shard_map(local, mesh=mesh, in_specs=in_specs, out_specs=out_specs, check_vma=False)
```

```python
import functools
import math

import jax
import jax.numpy as jnp
from jax import lax
from jax.experimental import pallas as pl
from jax.experimental.pallas import tpu as pltpu
from jax.sharding import PartitionSpec as P

HD = 128
H = 64
KVH = 4
GH = H // KVH
CORE_H = H // 2
CORE_GH = GH // 2

lowest = -1e30
rope_base = 500000.0
score_scale = 1.0 / math.sqrt(HD)
bf16 = jnp.bfloat16
f32 = jnp.float32
VMEM = pltpu.MemorySpace.VMEM
SMEM = pltpu.MemorySpace.SMEM
KV = KVH * HD
PAGE = 128
HALF = HD // 2


def rotate(vectors, cosine, sine):
    return vectors * cosine + pltpu.roll(vectors, HALF, 1) * sine


def exchange(buffer):
    chips = buffer.shape[0]
    groups = [[2 * chip + core for chip in range(chips)] for core in range(2)]
    return lax.all_to_all(buffer, "attn", 0, 0, tiled=True, axis_index_groups=groups)


def swap_cores(buffer):
    n = lax.axis_size("attn")
    return lax.ppermute(buffer, "attn", [(i, i ^ 1) for i in range(n)])


def lane_of(shape):
    return lax.broadcasted_iota(jnp.int32, shape, 1)


def spread_kernel(device, hidden, send):
    for j in range(send.shape[0]):
        send[j] = hidden[...]


def add_kernel(got, entries, out, new_entries):
    total = got[0].astype(f32)
    for src in range(1, got.shape[0]):
        total = total + got[src].astype(f32)
    out[...] = total.astype(bf16)
    requests = out.shape[0]
    for i in range(2 * KVH):
        rows = slice(i * requests, (i + 1) * requests)
        new_entries[:, i * HD : (i + 1) * HD] = entries[rows, :].astype(bf16)


def place_slots(device, lengths, table, placed, slots, total):
    requests = table.shape[0]
    lane = lane_of((1, HD))
    partner = device + 1 - 2 * lax.rem(device, 2)
    slot = jnp.where(lane < slots, device * slots + lane, (partner - 1) * slots + lane)
    pair = jnp.full((1, HD), requests * KVH, jnp.int32)
    alive = jnp.zeros((1, HD), jnp.int32)
    for r in range(requests):
        pages = lax.div(lengths[r] + PAGE - 1, PAGE)
        offset = slot - table[r, 0, 0]
        offset = jnp.where(offset < 0, offset + total, offset)
        here = offset < KVH * pages
        group = jnp.zeros((1, HD), jnp.int32)
        for g in range(1, KVH):
            group = group + (offset >= g * pages).astype(jnp.int32)
        pair = jnp.where(here, r * KVH + group, pair)
        alive = jnp.where(here, lengths[r] - 1 - (offset - group * pages) * PAGE, alive)
    placed[0:1, :] = pair
    placed[1:2, :] = alive


def prepare_kernel(
    device, lengths, table, near, tables, own_tables, placed, square, *, slots
):
    chips, requests, _ = near.shape
    total = jnp.zeros(square.shape, f32)
    for chip in range(chips):
        values = near[chip].astype(f32)
        total = total + values * values
    square[...] = total
    row, lane = lax.broadcasted_iota(jnp.int32, (requests, HD), 0), lane_of((requests, HD))
    position = jnp.zeros((requests, HD), f32)
    for r in range(requests):
        position = jnp.where(row == r, (lengths[r] - 1).astype(f32), position)
    index = jnp.where(lane < HALF, lane, lane - HALF).astype(f32)
    angles = position * jnp.exp(index * (-2.0 * math.log(rope_base) / HD))
    sine = jnp.sin(angles)
    tables[:requests] = jnp.cos(angles)
    tables[requests:] = jnp.where(lane < HALF, -sine, sine)
    mine = lax.div(device[0], 2)
    keys_here = lax.rem(device[0], 2) == 0
    own_tables[0:1, :] = jnp.where(keys_here, tables[pl.ds(mine, 1), :], 1.0)
    own_tables[1:2, :] = jnp.where(keys_here, tables[pl.ds(requests + mine, 1), :], 0.0)
    place_slots(device[0], lengths, table, placed, slots, 2 * chips * slots)


def normalize_kernel(device, near, far, square, gain, w_kv, normed, kept, away):
    chips, requests, width = near.shape
    n = 2 * chips
    core = lax.rem(device[0], 2)
    total = square[...]
    for chip in range(chips):
        values = far[chip].astype(f32)
        total = total + values * values
    scale = lax.rsqrt(jnp.sum(total, axis=1, keepdims=True) / (n * width) + 1e-05)
    for k in range(n):
        chip, from_core = divmod(k, 2)
        values = jnp.where(core == from_core, near[chip].astype(f32), far[chip].astype(f32))
        normed[k] = (values * scale * gain[:, k * width : (k + 1) * width]).astype(bf16)
    own = normed[device[0]]
    for result, half in ((kept, core), (away, 1 - core)):
        columns = pl.ds(pl.multiple_of(half * KV, KV), KV)
        result[...] = jnp.dot(own, w_kv[:, columns], preferred_element_type=f32)


def query_kernel(normed, tables, w_query, query):
    n, requests, width = normed.shape
    columns = w_query.shape[1]
    product = jnp.zeros((requests, columns), f32)
    for k in range(n):
        product = product + jnp.dot(
            normed[k], w_query[k * width : (k + 1) * width, :], preferred_element_type=f32
        )
    cosine, sine = tables[:requests], tables[requests:]
    for c in range(columns // HD):
        turned = rotate(product[:, c * HD : (c + 1) * HD], cosine, sine)
        query[:, c * HD : (c + 1) * HD] = turned.astype(bf16)


def gather_kernel(query, kept, came, send, kv_rows):
    chips, requests, wide = send.shape
    columns = wide - HD
    for group in range(KVH):
        part = slice(group * HD, (group + 1) * HD)
        value = kept[:, part] + came[:, part]
        upper = value.astype(bf16).astype(f32)
        kv_rows[pl.ds(group, requests, stride=2 * KVH), :] = upper
        kv_rows[pl.ds(KVH + group, requests, stride=2 * KVH), :] = value - upper
    whole = query[...]
    for chip in range(chips):
        send[chip, :, :columns] = whole
        rows = kv_rows[chip * 2 * KVH : (chip + 1) * 2 * KVH, :]
        if requests > 2 * KVH:
            rows = jnp.concatenate([rows, jnp.zeros((requests - 2 * KVH, HD), f32)], axis=0)
        send[chip, :, columns:] = rows.astype(bf16)


def entry_kernel(got, own_tables, row):
    columns = got.shape[2] - HD
    kv = jnp.zeros((2 * KVH, HD), f32)
    for chip in range(got.shape[0]):
        kv = kv + got[chip, : 2 * KVH, columns:].astype(f32)
    kv = kv + pltpu.roll(kv, KVH, 0)
    row[...] = rotate(kv, own_tables[0:1, :], own_tables[1:2, :]).astype(bf16)


def attend_kernel(
    placed, got, k_near, v_near, k_far, v_far, peak, total, mixed,
    queries, slot_score, slot_out, slot_peak, slot_total, run_peak, run_total, run_mixed,
):
    chips, requests, wide = got.shape
    heads = (wide - HD) // HD
    slots, page = k_near.shape[:2]
    pairs = requests * KVH
    for h in range(CORE_H):
        chip, c = divmod(h, heads)
        queries[pl.ds(h, requests, stride=CORE_H), :] = got[
            chip, :, c * HD : (c + 1) * HD
        ].astype(f32)
    queries[pairs * CORE_GH :, :] = jnp.zeros((CORE_GH, HD), f32)
    run_peak[...] = jnp.full_like(run_peak, lowest)
    run_total[...] = jnp.zeros_like(run_total)
    run_mixed[...] = jnp.zeros_like(run_mixed)

    def rows_of(s, side=0):
        start = (placed[0, s] + side * (pairs + 1)) * CORE_GH
        return pl.ds(pl.multiple_of(start, CORE_GH), CORE_GH)

    for s in range(0, 2 * slots, 2):
        pages, at = (k_near, s) if s < slots else (k_far, s - slots)
        both = jnp.concatenate([queries[rows_of(s), :], queries[rows_of(s + 1), :]], axis=0)
        scores = lax.dot_general(
            both.astype(bf16), pages[at : at + 2].reshape(2 * page, HD), (((1,), (1,)), ((), ())),
            preferred_element_type=f32,
        )
        slot_score[s] = scores[:CORE_GH, :page]
        slot_score[s + 1] = scores[CORE_GH:, page:]
    shape = (CORE_GH, HD)
    places = lane_of((CORE_GH, page))
    for s in range(2 * slots):
        alive = places < placed[1, s]
        scores = jnp.where(alive, slot_score[s] * score_scale, lowest)
        top = jnp.max(scores, axis=1, keepdims=True)
        weights = jnp.where(alive, jnp.exp(scores - top), 0.0)
        slot_score[s] = weights
        slot_peak[s] = jnp.broadcast_to(top, shape)
        slot_total[s] = jnp.broadcast_to(jnp.sum(weights, axis=1, keepdims=True), shape)
    nothing = jnp.zeros((CORE_GH, page), f32)
    for s in range(0, 2 * slots, 2):
        pages, at = (v_near, s) if s < slots else (v_far, s - slots)
        upper = jnp.concatenate([slot_score[s], nothing], axis=1)
        lower = jnp.concatenate([nothing, slot_score[s + 1]], axis=1)
        both = jnp.concatenate([upper, lower], axis=0).astype(bf16)
        out = jnp.dot(
            both, pages[at : at + 2].reshape(2 * page, HD), preferred_element_type=f32
        )
        slot_out[s] = out[:CORE_GH]
        slot_out[s + 1] = out[CORE_GH:]
    running = [jnp.full(shape, lowest, f32)] * 2
    for t in range(slots):
        for side in range(2):
            s = side * slots + t
            if t:
                same = placed[0, s] == placed[0, s - 1]
                running[side] = jnp.where(same, running[side], lowest)
            running[side] = jnp.maximum(slot_peak[s], running[side])
            run_peak[rows_of(s, side), :] = running[side]
    for s in range(2 * slots):
        slot_peak[s] = jnp.exp(slot_peak[s] - run_peak[rows_of(s, s // slots), :])
    sum_total = [jnp.zeros(shape, f32)] * 2
    sum_mixed = [jnp.zeros(shape, f32)] * 2
    for t in range(slots):
        for side in range(2):
            s = side * slots + t
            if t:
                keep = jnp.where(placed[0, s] == placed[0, s - 1], 1.0, 0.0)
                sum_total[side], sum_mixed[side] = keep * sum_total[side], keep * sum_mixed[side]
            rows, factor = rows_of(s, side), slot_peak[s]
            sum_total[side] = sum_total[side] + factor * slot_total[s]
            sum_mixed[side] = sum_mixed[side] + factor * slot_out[s]
            run_total[rows, :] = sum_total[side]
            run_mixed[rows, :] = sum_mixed[side]
    for pair in range(pairs):
        here = slice(pair * CORE_GH, (pair + 1) * CORE_GH)
        first = run_peak[here, :]
        there = slice((pairs + 1 + pair) * CORE_GH, (pairs + 2 + pair) * CORE_GH)
        second = run_peak[there, :]
        top = jnp.maximum(first, second)
        first, second = jnp.exp(first - top), jnp.exp(second - top)
        peak[here, :] = top
        total[here, :] = first * run_total[here, :] + second * run_total[there, :]
        mixed[here, :] = first * run_mixed[here, :] + second * run_mixed[there, :]


def share_kernel(device, peak, total, mixed, near_row, far_row, send, kv_block):
    chips, requests, wide = send.shape
    columns = wide - 2 * HD
    heads = columns // HD
    core = lax.rem(device[0], 2)
    near, far = near_row[...].astype(f32), far_row[...].astype(f32)
    keys_here = lax.broadcasted_iota(jnp.int32, near.shape, 0) < KVH
    own = jnp.where(core == 0, near, far)
    other = jnp.where(core == 0, far, near)
    if requests > 2 * KVH:
        kv_block[...] = jnp.zeros_like(kv_block)
    kv_block[: 2 * KVH, :] = jnp.where(keys_here, own, other)
    lanes = lane_of((requests, HD))
    order = lax.rem(lanes, heads)
    kind = lax.div(lanes, heads)
    kinds = lax.rem(kind, 3)
    for chip in range(chips):
        stats = jnp.zeros((requests, HD), f32)
        for c in range(heads):
            rows = pl.ds(chip * heads + c, requests, stride=CORE_H)
            send[chip, :, c * HD : (c + 1) * HD] = mixed[rows, :].astype(bf16)
            value = jnp.where(kind < 3, peak[rows, :], total[rows, :])
            stats = jnp.where(order == c, value, stats)
        first = stats.astype(bf16).astype(f32)
        stats = stats - first
        second = stats.astype(bf16).astype(f32)
        third = stats - second
        stats = jnp.where(kinds == 0, first, jnp.where(kinds == 1, second, third))
        send[chip, :, columns : columns + HD] = stats.astype(bf16)
        send[chip, :, columns + HD :] = kv_block[...].astype(bf16)


def multiply_out(attention, w_out, result, core):
    chips, _, width = result.shape
    whole = attention[...]
    for chip in range(chips):
        columns = pl.ds(pl.multiple_of((2 * chip + core) * width, HD), width)
        result[chip] = jnp.dot(
            whole, w_out[:, columns], preferred_element_type=f32
        ).astype(result.dtype)


def combine_kernel(device, got, query, w_out, away, attention, entries):
    chips, requests, wide = got.shape
    columns = wide - 2 * HD
    heads = columns // HD
    lanes = lane_of((requests, HD))
    for request in range(requests):
        block = got[request, : 2 * KVH, columns + HD :].astype(f32)
        entries[pl.ds(request, 2 * KVH, stride=requests), :] = block

    def own(c, half):
        start = (lax.div(device[0] * heads + c, GH) + half * KVH) * requests
        return entries[pl.ds(pl.multiple_of(start, 8), requests), :]

    new_score = jnp.full((requests, HD), lowest, f32)
    for c in range(heads):
        score = query[:, c * HD : (c + 1) * HD].astype(f32) * own(c, 0)
        score = jnp.sum(score, axis=1, keepdims=True) * score_scale
        new_score = jnp.where(lanes == c, score, new_score)
    peaks, totals = [], []
    for src in range(chips):
        stats = got[src, :, columns : columns + HD].astype(f32)
        stats = (
            stats + pltpu.roll(stats, HD - heads, 1) + pltpu.roll(stats, HD - 2 * heads, 1)
        )
        peaks.append(stats)
        totals.append(pltpu.roll(stats, HD - 3 * heads, 1))
    top = new_score
    for value in peaks:
        top = jnp.maximum(top, value)
    weights = [jnp.exp(value - top) for value in peaks]
    new_weight = jnp.exp(new_score - top)
    total = new_weight
    for weight, value in zip(weights, totals):
        total = total + weight * value
    inverse = 1.0 / total
    weights = [weight * inverse for weight in weights]
    new_weight = new_weight * inverse
    for c in range(heads):
        mixed = new_weight[:, c : c + 1] * own(c, 1)
        for src in range(chips):
            mixed = mixed + weights[src][:, c : c + 1] * got[
                src, :, c * HD : (c + 1) * HD
            ].astype(f32)
        attention[:, c * HD : (c + 1) * HD] = mixed.astype(bf16)
    multiply_out(attention, w_out, away, 1 - lax.rem(device[0], 2))


def keep_kernel(device, attention, w_out, kept):
    multiply_out(attention, w_out, kept, lax.rem(device[0], 2))


def join_kernel(kept, came, send):
    for chip in range(send.shape[0]):
        send[chip] = (kept[chip] + came[chip].astype(f32)).astype(bf16)


def call(kernel, out_shape, in_spaces, out_spaces, scratch, limit, moved=None):
    return pl.pallas_call(
        kernel,
        out_shape=out_shape,
        in_specs=[pl.BlockSpec(memory_space=space) for space in in_spaces],
        out_specs=[pl.BlockSpec(memory_space=space) for space in out_spaces],
        scratch_shapes=scratch,
        compiler_params=pltpu.CompilerParams(vmem_limit_bytes=limit << 20),
        cost_estimate=moved
        and pl.CostEstimate(flops=moved * 512, bytes_accessed=moved, transcendentals=0),
    )


def local(hidden, gain, w_query, w_kv, w_out, k_cache, v_cache, block_table, lengths):
    device = lax.axis_index("attn").astype(jnp.int32).reshape(1)
    n = lax.axis_size("attn")
    requests, width = hidden.shape
    columns = w_query.shape[1]
    slots = k_cache.shape[0]
    pairs = requests * KVH
    assert 2 * requests == n and slots % 2 == 0 and 2 * slots <= HD

    shape = jax.ShapeDtypeStruct
    halves = shape((n // 2, requests, width), bf16)
    device, k_cache, v_cache = lax.optimization_barrier((device, k_cache, v_cache))
    k_far, v_far = swap_cores(k_cache), swap_cores(v_cache)
    (send,) = call(
        spread_kernel,
        [halves],
        [SMEM, VMEM],
        [VMEM],
        [],
        2,
        2 * (w_query.nbytes + w_kv.nbytes),
    )(device, hidden)
    near = exchange(send)
    far = swap_cores(near)
    tables, own_tables, placed, square = call(
        functools.partial(prepare_kernel, slots=slots),
        [
            shape((2 * requests, HD), f32),
            shape((2, HD), f32),
            shape((2, HD), jnp.int32),
            shape((requests, width), f32),
        ],
        [SMEM] * 3 + [VMEM],
        [VMEM] * 4,
        [],
        2,
    )(device, lengths, block_table, near)
    half_kv = shape((requests, KV), f32)
    normed, kept, away = call(
        normalize_kernel,
        [shape((n, requests, width), bf16), half_kv, half_kv],
        [SMEM] + [VMEM] * 5,
        [VMEM] * 3,
        [],
        4,
    )(device, near, far, square, gain.reshape(1, n * width), w_kv)
    came = swap_cores(away)
    (query,) = call(
        query_kernel, [shape((requests, columns), bf16)], [VMEM] * 3, [VMEM], [], 4
    )(normed, tables, w_query)
    (send,) = call(
        gather_kernel,
        [shape((n // 2, requests, columns + HD), bf16)],
        [VMEM] * 3,
        [VMEM],
        [pltpu.VMEM((requests * 2 * KVH, HD), f32)],
        4,
    )(query, kept, came)
    got = exchange(send)
    (near_row,) = call(entry_kernel, [shape((2 * KVH, HD), bf16)], [VMEM] * 2, [VMEM], [], 2)(
        got, own_tables
    )
    far_row = swap_cores(near_row)
    rows = shape((pairs * CORE_GH, HD), f32)
    slot_rows = pltpu.VMEM((2 * slots, CORE_GH, HD), f32)
    run_rows = pltpu.VMEM((2 * (pairs + 1) * CORE_GH, HD), f32)
    peak, total, mixed = call(
        attend_kernel,
        [rows] * 3,
        [SMEM] + [VMEM] * 5,
        [VMEM] * 3,
        [pltpu.VMEM(((pairs + 1) * CORE_GH, HD), f32)] + [slot_rows] * 4 + [run_rows] * 3,
        8,
    )(placed, got, k_cache, v_cache, k_far, v_far)
    (send,) = call(
        share_kernel,
        [shape((n // 2, requests, columns + 2 * HD), bf16)],
        [SMEM] + [VMEM] * 5,
        [VMEM],
        [pltpu.VMEM((requests, HD), f32)],
        4,
    )(device, peak, total, mixed, near_row, far_row)
    got = exchange(send)
    away, attention, entries = call(
        combine_kernel,
        [
            halves,
            shape((requests, columns), bf16),
            shape((2 * KVH * requests, HD), f32),
        ],
        [SMEM] + [VMEM] * 3,
        [VMEM] * 3,
        [],
        4,
    )(device, got, query, w_out)
    came = swap_cores(away)
    (kept,) = call(
        keep_kernel, [shape(halves.shape, f32)], [SMEM] + [VMEM] * 2, [VMEM], [], 4
    )(device, attention, w_out)
    (send,) = call(join_kernel, [halves], [VMEM] * 2, [VMEM], [], 4)(kept, came)
    got = exchange(send)
    attn_out, new_entries = call(
        add_kernel,
        [shape((requests, width), bf16), shape((requests, 2 * KV), bf16)],
        [VMEM] * 2,
        [VMEM] * 2,
        [],
        4,
    )(got, entries)
    return attn_out, new_entries


def solution(mesh):
    in_specs = (
        P("groups", "attn"),
        P(),
        P(None, "attn"),
        P("attn", None),
        P("attn", None),
        P(("groups", "attn"), None, None),
        P(("groups", "attn"), None, None),
        P("groups", None, None),
        P("groups"),
    )
    out_specs = (P("groups", "attn"), P("groups", None))
    return jax.shard_map(local, mesh=mesh, in_specs=in_specs, out_specs=out_specs, check_vma=False)
```
